32 devices in a mesh: groups: 2 (over x), tensor: 16 (over z, y, core).
Axes of the slice: x: 2, y: 2, z: 4, core: 2. Of those that a mesh axis runs over, the one named last changes fastest.
Arguments:
- hidden: bfloat16 [512, 8192], P('groups', 'tensor'), parts along dimension 0, may hold values from -6 to 6
- attention_norm_gain: bfloat16 [8192], replicated, may hold values from 0.099609375 to 1.8984375
- query_weight: bfloat16 [8192, 8192], P(None, 'tensor'), may hold values from -0.0625 to 0.0625
- key_value_weight: bfloat16 [8192, 2048], P(None, 'tensor'), may hold values from -0.0625 to 0.0625
- output_weight: bfloat16 [8192, 8192], P(None, 'tensor'), may hold values from -0.5 to 0.5
- adapter_down_factors: bfloat16 [64, 8192, 64], P(None, 'tensor'), may hold values from -0.0625 to 0.0625
- adapter_query_up: bfloat16 [64, 64, 8192], P(None, None, 'tensor'), may hold values from -0.75 to 0.75
- adapter_key_value_up: bfloat16 [64, 64, 2048], P(None, None, 'tensor'), may hold values from -0.75 to 0.75
- output_adapter_down: bfloat16 [64, 8192, 64], P(None, 'tensor'), may hold values from -0.5 to 0.5
- output_adapter_up: bfloat16 [64, 64, 8192], P(None, None, 'tensor'), may hold values from -0.75 to 0.75
- key_cache: bfloat16 [4096, 512, 128], P(('groups', 'tensor')), parts along dimension 0, as said below
- value_cache: bfloat16 [4096, 512, 128], P(('groups', 'tensor')), parts along dimension 0, may hold values from -6 to 6
- adapter: int32 [512, 1], P('groups'), parts along dimension 0, may hold values from 0 to 63
- lengths: int32 [512], P('groups'), parts along dimension 0, may hold values from 1 to 512, as said below
Outputs:
- result: bfloat16 [512, 8192], P('groups', 'tensor'), parts along dimension 0
The draws below stay inside these ranges and needn't reach their ends.
There are 2 independent parts, one for each index of `groups`. The reference program is written for one: setup_inputs(seed, part) draws one part's arguments, and reference() takes and returns one part's arrays. A program takes and returns all parts, laid end to end along the dimension named above; an argument that names none is the same for every part. Nothing has to cross between parts.
Inputs may be any that keep to these rules, and one draw needn't show every extreme that they name: Each row attends to its first lengths positions of the cache and to its new token, which stands at position lengths; some row has exactly 512 and some row 1. Every adapter serves at least one row. `key_cache`: keys are stored already rotated.
All inputs are finite; a program needn't handle non-finite values.
Results may differ from the reference program's by a relative error of at most 0.007.
The reference program's roundings to bfloat16 on the way count: a program that leaves them out, or rounds other values in their place, can miss the bound.
Values may be sent and summed in bfloat16 or wider, within the bound.
A program may use at most 192 MiB of HBM per device.

```python
import jax
import jax.numpy as jnp
from jax import lax

MODEL_WIDTH = 8192
QUERY_HEADS = 64
KEY_VALUE_HEADS = 8
HEAD_SIZE = 128
ADAPTER_COUNT = 64
ADAPTER_RANK = 64
ROWS = 256
CACHE = 512


def draw_key_cache(key, part):
    key = jax.random.fold_in(key, 7)
    normal_part = jnp.clip(jax.random.normal(key, (KEY_VALUE_HEADS * ROWS, CACHE, HEAD_SIZE), jnp.float32), -6.0, 6.0)
    return normal_part.astype(jnp.bfloat16)


def draw_lengths(key, part):
    key = jax.random.fold_in(key, 13)
    first_key = jax.random.fold_in(key, 1)
    second_key = jax.random.fold_in(key, 2)
    drawn = jax.random.randint(first_key, (ROWS,), 1, CACHE + 1, jnp.int32)
    chosen_row = jax.random.randint(second_key, (), 0, ROWS, jnp.int32)
    row_index = jnp.arange(ROWS, dtype=jnp.int32)
    drawn = jnp.where(row_index == chosen_row, CACHE, drawn)
    drawn = jnp.where(row_index == (chosen_row + 1) % ROWS, 1, drawn)
    return drawn.astype(jnp.int32)


def shard_levels(key, shape, pieces, least, top_value):
    factor_of = 1.0
    for dim, shards_of in pieces:
        steps = jax.random.uniform(jax.random.fold_in(jax.random.fold_in(key, 6), dim), (shards_of,), jnp.float32, least / len(pieces), top_value / len(pieces))
        factor_of = factor_of * jnp.repeat(jnp.exp(steps), shape[dim] // shards_of).reshape((-1,) + (1,) * (len(shape) - 1 - dim))
    return factor_of


def different_ones(own_key, rows, amount, top, lift):
    order = jax.random.permutation(jax.random.fold_in(own_key, 1), amount)
    pull = order
    for power in range(3):
        pull = pull * pull // amount
    pull = pull * lift // amount
    tickets = jax.random.randint(jax.random.fold_in(own_key, 2), (rows, amount), 0, 4096) + pull
    sure = jax.random.permutation(jax.random.fold_in(own_key, 3), rows)[jnp.arange(amount) % rows]
    tickets = jnp.where(jnp.arange(rows)[:, None] == sure[None, :], 1 << 14, tickets)
    merit = tickets * amount + jnp.arange(amount)
    return lax.top_k(merit.astype(jnp.int32), top)[1].astype(jnp.int32)


def gaussian(key, dims, width, reach, split=(), kind=jnp.bfloat16):
    level = shard_levels(key, dims, split, -0.22, 0.18) if split else 1.0
    values = jax.random.normal(key, dims, jnp.float32) * width * level
    return jnp.minimum(jnp.maximum(values, -reach), reach).astype(kind)


def setup_inputs(seed: int = 0, part: int = 0) -> dict:
    key_list = jax.random.split(jax.random.key(seed), 15)
    part_keys = jax.random.split(jax.random.fold_in(key_list[14], part), 15)
    hidden = gaussian(part_keys[0], (ROWS, MODEL_WIDTH), 1.0, 6.0, ((1, 16),))
    attention_norm_gain = jnp.clip(1.0 + 0.18 * jax.random.normal(key_list[1], (MODEL_WIDTH,), jnp.float32), 0.099609375, 1.8984375).astype(jnp.bfloat16)
    query_weight = gaussian(key_list[2], (MODEL_WIDTH, QUERY_HEADS * HEAD_SIZE), MODEL_WIDTH ** -0.5, 0.0625, ((1, 16),))
    key_value_weight = gaussian(key_list[3], (MODEL_WIDTH, 2 * KEY_VALUE_HEADS * HEAD_SIZE), MODEL_WIDTH ** -0.5, 0.0625, ((1, 16),))
    output_weight = gaussian(key_list[4], (QUERY_HEADS * HEAD_SIZE, MODEL_WIDTH), (QUERY_HEADS * HEAD_SIZE // 64) ** -0.5, 0.5, ((1, 16),))
    adapter_down_factors = gaussian(key_list[5], (ADAPTER_COUNT, MODEL_WIDTH, ADAPTER_RANK), MODEL_WIDTH ** -0.5, 0.0625, ((1, 16),))
    adapter_query_up = gaussian(key_list[6], (ADAPTER_COUNT, ADAPTER_RANK, QUERY_HEADS * HEAD_SIZE), ADAPTER_RANK ** -0.5, 0.75, ((2, 16),))
    adapter_key_value_up = gaussian(key_list[7], (ADAPTER_COUNT, ADAPTER_RANK, 2 * KEY_VALUE_HEADS * HEAD_SIZE), ADAPTER_RANK ** -0.5, 0.75, ((2, 16),))
    output_adapter_down = gaussian(key_list[8], (ADAPTER_COUNT, QUERY_HEADS * HEAD_SIZE, ADAPTER_RANK), (QUERY_HEADS * HEAD_SIZE // 64) ** -0.5, 0.5, ((1, 16),))
    output_adapter_up = gaussian(key_list[9], (ADAPTER_COUNT, ADAPTER_RANK, MODEL_WIDTH), ADAPTER_RANK ** -0.5, 0.75, ((2, 16),))
    key_cache = draw_key_cache(jax.random.fold_in(jax.random.fold_in(key_list[14], part), 71), part)
    value_cache = gaussian(part_keys[11], (KEY_VALUE_HEADS * ROWS, CACHE, HEAD_SIZE), 1.0, 6.0, ((0, 16),))
    adapter = different_ones(part_keys[12], ROWS, ADAPTER_COUNT, 1, 256)
    lengths = draw_lengths(jax.random.fold_in(jax.random.fold_in(key_list[14], part), 71), part)
    return dict(hidden=hidden, attention_norm_gain=attention_norm_gain, query_weight=query_weight, key_value_weight=key_value_weight, output_weight=output_weight, adapter_down_factors=adapter_down_factors, adapter_query_up=adapter_query_up, adapter_key_value_up=adapter_key_value_up, output_adapter_down=output_adapter_down, output_adapter_up=output_adapter_up, key_cache=key_cache, value_cache=value_cache, adapter=adapter, lengths=lengths)


adapter_scale = 0.5
rope_base = 500000.0
norm_eps = 1e-05

def rotate(values, positions):
    half_width = values.shape[-1] // 2
    frequency = rope_base ** (-(jnp.arange(half_width, dtype=jnp.float32) * 2.0) / values.shape[-1])
    angles = positions.astype(jnp.float32)[:, None, None] * frequency[None, None, :]
    cosine = jnp.cos(angles)
    sinus_part = jnp.sin(angles)
    front = values[..., :half_width]
    behind = values[..., half_width:]
    return jnp.concatenate([front * cosine - behind * sinus_part, front * sinus_part + behind * cosine], axis=-1)

def stored_entries(values):
    return lax.optimization_barrier(values.astype(jnp.bfloat16))

def reference(hidden, attention_norm_gain, query_weight, key_value_weight, output_weight, adapter_down_factors, adapter_query_up, adapter_key_value_up, output_adapter_down, output_adapter_up, key_cache, value_cache, adapter, lengths):
    stream = hidden.astype(jnp.float32)
    mean_square = lax.optimization_barrier(jnp.mean(stream * stream, axis=1, keepdims=True))
    normed_input = (stream * lax.rsqrt(mean_square + norm_eps) * attention_norm_gain.astype(jnp.float32)[None, :]).astype(jnp.bfloat16)
    chosen_adapter = adapter[:, 0:1] == jnp.arange(ADAPTER_COUNT, dtype=jnp.int32)[None, :]

    def project_down(inputs, table):
        spread = jnp.einsum('rd,adk->rak', inputs.astype(jnp.float32), table.astype(jnp.float32))
        return lax.optimization_barrier(jnp.sum(jnp.where(chosen_adapter[:, :, None], spread, 0.0), axis=1))

    def project_upward(low_values, table):
        expanded = jnp.where(chosen_adapter[:, :, None], low_values.astype(jnp.float32)[:, None, :], 0.0)
        return jnp.einsum('rak,akc->rc', expanded, table.astype(jnp.float32))
    reduced_input = stored_entries(project_down(normed_input, adapter_down_factors))
    query_vector = jnp.dot(normed_input, query_weight, preferred_element_type=jnp.float32) + adapter_scale * project_upward(reduced_input, adapter_query_up)
    query_vector = stored_entries(rotate(query_vector.reshape(ROWS, QUERY_HEADS, HEAD_SIZE), lengths))
    fresh_entries = jnp.dot(normed_input, key_value_weight, preferred_element_type=jnp.float32) + adapter_scale * project_upward(reduced_input, adapter_key_value_up)
    fresh_entries = stored_entries(fresh_entries).reshape(ROWS, KEY_VALUE_HEADS, 2, HEAD_SIZE)
    new_key = stored_entries(rotate(fresh_entries[:, :, 0, :].astype(jnp.float32), lengths))
    new_value = fresh_entries[:, :, 1, :].astype(jnp.float32)
    group_heads = QUERY_HEADS // KEY_VALUE_HEADS
    queries = jnp.transpose(query_vector.astype(jnp.float32).reshape(ROWS, group_heads, KEY_VALUE_HEADS, HEAD_SIZE), (0, 2, 1, 3))
    keys = key_cache.astype(jnp.float32).reshape(KEY_VALUE_HEADS, ROWS, CACHE, HEAD_SIZE)
    values = value_cache.astype(jnp.float32).reshape(KEY_VALUE_HEADS, ROWS, CACHE, HEAD_SIZE)
    factor = HEAD_SIZE ** (-0.5)
    scores = jnp.einsum('rkgd,krpd->rkgp', queries, keys) * factor
    live = jnp.arange(CACHE, dtype=jnp.int32)[None, :] < lengths[:, None]
    scores = jnp.where(live[:, None, None, :], scores, -jnp.inf)
    own_score = jnp.einsum('rkgd,rkd->rkg', queries, new_key.astype(jnp.float32)) * factor
    joined = jnp.concatenate([scores, own_score[..., None]], axis=-1)
    probs = stored_entries(jax.nn.softmax(joined, axis=-1)).astype(jnp.float32)
    attended_rows = jnp.einsum('rkgp,krpd->rkgd', probs[..., :CACHE], values)
    attended_rows = attended_rows + probs[..., CACHE:] * new_value[:, :, None, :]
    attended_rows = stored_entries(attended_rows.reshape(ROWS, QUERY_HEADS * HEAD_SIZE))
    reduced_output = stored_entries(project_down(attended_rows, output_adapter_down))
    block_output = stream + jnp.dot(attended_rows, output_weight, preferred_element_type=jnp.float32)
    block_output = block_output + adapter_scale * project_upward(reduced_output, output_adapter_up)
    return block_output.astype(jnp.bfloat16)
```

```python
import functools

import jax
import jax.numpy as jnp
from jax import lax
from jax.experimental import pallas as pl
from jax.experimental.pallas import tpu as pltpu
from jax.sharding import PartitionSpec as P

QUERY_HEADS = 64
KEY_VALUE_HEADS = 8
HEAD_SIZE = 128
GROUP_HEADS = QUERY_HEADS // KEY_VALUE_HEADS

adapter_scale = 0.5
rope_base = 500000.0
norm_eps = 1e-05

MESH = pl.DeviceIdType.MESH
F32 = jnp.float32
BF16 = jnp.bfloat16
NT = (((1,), (1,)), ((), ()))


def remote(src, dst, send_sem, recv_sem, peer):
    return pltpu.make_async_remote_copy(
        src_ref=src,
        dst_ref=dst,
        send_sem=send_sem,
        recv_sem=recv_sem,
        device_id={"tensor": peer},
        device_id_type=MESH,
    )


def greet_all(n, me):
    barrier = pltpu.get_barrier_semaphore()

    def greet(i, carry):
        pl.semaphore_signal(
            barrier, inc=1, device_id={"tensor": lax.rem(me + i, n)}, device_id_type=MESH
        )
        return carry

    lax.fori_loop(1, n, greet, 0)
    pl.semaphore_wait(barrier, n - 1)


def for_peers(n, me, action):
    def step(i, carry):
        action(i, lax.rem(me + i, n))
        return carry

    lax.fori_loop(1, n, step, 0)


class Exchange:
    def __init__(self, n, me, buf, send, recv, source):
        self.n, self.me, self.buf, self.send, self.recv, self.source = n, me, buf, send, recv, source

    def copy(self, i, peer):
        return remote(
            self.source(peer), self.buf.at[self.me], self.send.at[i], self.recv.at[self.me], peer
        )

    def start(self):
        for_peers(self.n, self.me, lambda i, peer: self.copy(i, peer).start())

    def wait_arrived(self):
        def arrived(i, peer):
            remote(
                self.source(peer), self.buf.at[peer], self.send.at[i], self.recv.at[peer], peer
            ).wait_recv()

        for_peers(self.n, self.me, arrived)

    def wait_sent(self):
        for_peers(self.n, self.me, lambda i, peer: self.copy(i, peer).wait_send())


class Gather:
    def __init__(self, n, me, view, zsend, ysend, csend, recv):
        self.wide = 2 if n % 4 == 0 and n <= 16 else 1
        self.depth = n // (2 * self.wide)
        self.view, self.me = view, me
        self.zsend, self.ysend, self.csend, self.recv = zsend, ysend, csend, recv
        self.core = lax.rem(me, 2)
        self.side = lax.rem(me // 2, self.wide)
        self.level = me // (2 * self.wide)

    def index(self, level, side, core):
        return (level * self.wide + side) * 2 + core

    def copy(self, block, send_sem, peer):
        return remote(self.view(block), self.view(block), send_sem, self.recv.at[block], peer)

    def up(self, d):
        block = self.index(self.level - d, self.side, self.core)
        return self.copy(block, self.zsend.at[0, d], self.index(self.level + 1, self.side, self.core))

    def down(self, d):
        block = self.index(self.level + d, self.side, self.core)
        return self.copy(block, self.zsend.at[1, d], self.index(self.level - 1, self.side, self.core))

    def across(self, level, sem):
        block = self.index(level, self.side, self.core)
        return self.copy(block, self.ysend.at[sem], self.index(self.level, 1 - self.side, self.core))

    def over(self, level, side, sem):
        block = self.index(level, side, self.core)
        return self.copy(
            block, self.csend.at[side, sem], self.index(self.level, self.side, 1 - self.core)
        )

    def await_block(self, block, peer):
        self.copy(block, self.zsend.at[0, 0], peer).wait_recv()

    def each_sign(self, d, action):
        @pl.when(self.level - d >= 0)
        def _():
            action(self.level - d, 0)

        @pl.when((d > 0) & (self.level + d < self.depth))
        def _():
            action(self.level + d, 1)

    def line(self, d):
        def low(level, sign):
            @pl.when(d > 0)
            def _():
                other = self.level - 1 if sign == 0 else self.level + 1
                self.await_block(
                    self.index(level, self.side, self.core),
                    self.index(other, self.side, self.core),
                )

            if sign == 0:

                @pl.when(self.level + 1 < self.depth)
                def _():
                    self.up(d).start()

                @pl.when((d == 0) & (self.level > 0))
                def _():
                    self.down(d).start()

            else:

                @pl.when(self.level > 0)
                def _():
                    self.down(d).start()

            if self.wide == 2:
                self.across(level, 2 * d + sign).start()
            self.over(level, self.side, 2 * d + sign).start()

        self.each_sign(d, low)

    def rest(self, d):
        def take(level, sign):
            if self.wide == 2:
                self.await_block(
                    self.index(level, 1 - self.side, self.core),
                    self.index(self.level, 1 - self.side, self.core),
                )
                self.over(level, 1 - self.side, 2 * d + sign).start()

        self.each_sign(d, take)

        def other(level, sign):
            for side in range(self.wide):
                self.await_block(
                    self.index(level, side, 1 - self.core),
                    self.index(self.level, self.side, 1 - self.core),
                )

        self.each_sign(d, other)

    def wait_sent(self):
        def step(d, carry):
            def sent(level, sign):
                if sign == 0:

                    @pl.when(self.level + 1 < self.depth)
                    def _():
                        self.up(d).wait_send()

                    @pl.when((d == 0) & (self.level > 0))
                    def _():
                        self.down(d).wait_send()

                else:

                    @pl.when(self.level > 0)
                    def _():
                        self.down(d).wait_send()

                if self.wide == 2:
                    self.across(level, 2 * d + sign).wait_send()
                for side in range(self.wide):
                    self.over(level, side, 2 * d + sign).wait_send()

            self.each_sign(d, sent)
            return carry

        lax.fori_loop(0, self.depth, step, 0)

    def each_chip(self, d, action):
        def step(i, carry):
            level = jnp.where(i < self.wide, self.level - d, self.level + d)
            side = lax.rem(i, self.wide)

            @pl.when((level >= 0) & (level < self.depth) & ((i < self.wide) | (d > 0)))
            def _():
                action(level * self.wide + side)

            return carry

        lax.fori_loop(0, 2 * self.wide, step, 0)


def gather_semaphores(n):
    return [
        pltpu.SemaphoreType.DMA((2, n)),
        pltpu.SemaphoreType.DMA((2 * n,)),
        pltpu.SemaphoreType.DMA((2, 2 * n)),
        pltpu.SemaphoreType.DMA((n,)),
    ]


def low_partial(values, down, adapter, low):
    rank = HEAD_SIZE // 2
    lanes = lax.broadcasted_iota(jnp.int32, (values.shape[0], HEAD_SIZE), 1) // rank
    low[...] = jnp.zeros_like(low)
    width = 4 * HEAD_SIZE

    def step(i, carry):
        spread = lax.dot_general(
            values, down[pl.ds(pl.multiple_of(i * width, width), width), :], NT,
            preferred_element_type=F32,
        )
        total = low[...]
        for part in range(width // HEAD_SIZE):
            mine = adapter == lanes + (i * (width // rank) + part * (HEAD_SIZE // rank))
            total = total + jnp.where(mine, spread[:, part * HEAD_SIZE : (part + 1) * HEAD_SIZE], 0.0)
        low[...] = total
        return carry

    lax.fori_loop(0, down.shape[0] // width, step, 0)


def low_upward(low, tables, adapter, totals):
    rank = HEAD_SIZE // 2
    lanes = lax.broadcasted_iota(jnp.int32, low.shape, 1) // rank
    width = 4 * HEAD_SIZE

    def step(i, carry):
        parts = []
        for part in range(width // HEAD_SIZE):
            mine = adapter == lanes + (i * (width // rank) + part * (HEAD_SIZE // rank))
            parts.append(jnp.where(mine, low, 0.0).astype(BF16))
        spread = jnp.concatenate(parts, axis=1)
        at = pl.ds(pl.multiple_of(i * width, width), width)
        for table, total in zip(tables, totals):
            total[...] += adapter_scale * jnp.dot(spread, table[at, :], preferred_element_type=F32)
        return carry

    lax.fori_loop(0, tables[0].shape[0] // width, step, 0)


def reduce_low(n, me, pieces, low_all):
    total = pieces[0]
    for i in range(1, n):
        total = total + pieces[i]
    total = total + pltpu.roll(total, HEAD_SIZE // 2, 1)
    low_all[me] = total.astype(BF16).astype(F32)


def project_kernel(
    n,
    hidden, gain, adapter, cosine, sine, wq_hbm, wkv_hbm, down_hbm, upq_hbm, upkv_hbm,
    q_out, kv_out,
    buf, wq, wkv, down, upq, upkv, acc_q, acc_kv, stat, inv, own, low, pieces, low_all, q_cut, kv_cut,
    load_sem, zsend, ysend, csend, grecv, st_send, st_recv, rs_send, rs_recv, lo_send, lo_recv,
    q_send, q_recv, kv_send, kv_recv,
):
    me = lax.axis_index("tensor")
    rows, span = hidden.shape
    loads = [
        pltpu.make_async_copy(src, dst, load_sem.at[i])
        for i, (src, dst) in enumerate(
            [(down_hbm, down), (wq_hbm, wq), (wkv_hbm, wkv), (upq_hbm, upq), (upkv_hbm, upkv)]
        )
    ]
    buf[me] = hidden[...]
    greet_all(n, me)
    gather = Gather(n, me, lambda block: buf.at[block], zsend, ysend, csend, grecv)
    gather.line(0)
    for load in loads:
        load.start()

    own_values = hidden[...].astype(F32)
    squares = jnp.sum(own_values * own_values, axis=1, keepdims=True)
    stat[me] = jnp.transpose(jnp.broadcast_to(squares, (rows, HEAD_SIZE)))[:8, :]
    stats = Exchange(n, me, stat, st_send, st_recv, lambda peer: stat.at[me])
    stats.start()
    acc_q[...] = jnp.zeros_like(acc_q)
    acc_kv[...] = jnp.zeros_like(acc_kv)
    stats.wait_arrived()
    total = stat[0]
    for i in range(1, n):
        total = total + stat[i]
    mean = total[0:1, :] / (n * span)
    scale = lax.rsqrt(mean + norm_eps)
    inv[...] = jnp.transpose(jnp.broadcast_to(scale, (HEAD_SIZE, rows)))

    def normed(block):
        return (
            buf[block].astype(F32) * inv[:, 0:1] * gain[block].astype(F32)
        ).astype(BF16)

    who = adapter[...]
    own[...] = normed(me)
    loads[0].wait()
    low_partial(own[...], down, who, low)
    piece = rows // n
    pieces[me] = low[pl.ds(pl.multiple_of(me * piece, 8), piece), :]
    reduce = Exchange(
        n, me, pieces, rs_send, rs_recv,
        lambda peer: low.at[pl.ds(pl.multiple_of(peer * piece, 8), piece), :],
    )
    reduce.start()
    spread = Exchange(n, me, low_all, lo_send, lo_recv, lambda peer: low_all.at[me])
    loads[1].wait()
    loads[2].wait()
    loads[3].wait()
    loads[4].wait()

    def step(d, carry):
        @pl.when(d + 1 < gather.depth)
        def _():
            gather.line(d + 1)

        @pl.when(d == 1)
        def _():
            reduce.wait_arrived()
            reduce_low(n, me, pieces, low_all)
            spread.start()

        @pl.when(d == 2)
        def _():
            spread.wait_arrived()
            low_upward(low_all[...].reshape(rows, HEAD_SIZE), [upq, upkv], who, [acc_q, acc_kv])

        gather.rest(d)

        def chip_part(chip):
            for core in range(2):
                block = chip * 2 + core
                values = normed(block)
                at = pl.ds(pl.multiple_of(block * span, span), span)
                acc_q[...] += jnp.dot(values, wq[at, :], preferred_element_type=F32)
                acc_kv[...] += jnp.dot(values, wkv[at, :], preferred_element_type=F32)

        gather.each_chip(d, chip_part)
        return carry

    lax.fori_loop(0, gather.depth, step, 0)

    row_blocks = n // KEY_VALUE_HEADS
    block_rows = rows // row_blocks
    slots = acc_q.shape[1] // HEAD_SIZE
    cos, sin = cosine[...], sine[...]
    kv_cut[...] = acc_kv[...].astype(BF16)
    kv_group = me // row_blocks

    def kv_copy(part):
        peer = kv_group * row_blocks + part
        slot = lax.rem(me, row_blocks)
        return peer, slot, remote(
            kv_cut.at[pl.ds(part * block_rows, block_rows), :], kv_out.at[slot],
            kv_send.at[part], kv_recv.at[slot], peer,
        )

    def q_copy(i, part):
        column = me * slots + i
        peer = lax.rem(column, KEY_VALUE_HEADS) * row_blocks + part
        slot = column // KEY_VALUE_HEADS
        return peer, slot, remote(
            q_cut.at[i, pl.ds(part * block_rows, block_rows), :], q_out.at[slot],
            q_send.at[i, part], q_recv.at[slot], peer,
        )

    for part in range(row_blocks):
        peer, slot, copy = kv_copy(part)

        @pl.when(peer != me)
        def _():
            copy.start()

        @pl.when(peer == me)
        def _():
            kv_out[slot] = kv_cut[pl.ds(part * block_rows, block_rows), :]

    for i in range(slots):
        values = acc_q[:, i * HEAD_SIZE : (i + 1) * HEAD_SIZE]
        q_cut[i] = (values * cos + pltpu.roll(values, HEAD_SIZE // 2, 1) * sin).astype(BF16)
        for part in range(row_blocks):
            peer, slot, copy = q_copy(i, part)

            @pl.when(peer != me)
            def _():
                copy.start()

            @pl.when(peer == me)
            def _():
                q_out[slot] = q_cut[i, pl.ds(part * block_rows, block_rows), :]

    stats.wait_sent()
    reduce.wait_sent()
    spread.wait_sent()
    gather.wait_sent()
    for part in range(row_blocks):
        peer, slot, copy = kv_copy(part)

        @pl.when(peer != me)
        def _():
            copy.wait_send()
            remote(
                kv_cut.at[pl.ds(part * block_rows, block_rows), :], kv_out.at[part],
                kv_send.at[part], kv_recv.at[part], peer,
            ).wait_recv()

    for i in range(slots):
        for part in range(row_blocks):
            peer, slot, copy = q_copy(i, part)

            @pl.when(peer != me)
            def _():
                copy.wait_send()

    for slot in range(GROUP_HEADS):
        sender = (slot * KEY_VALUE_HEADS + kv_group) // slots

        @pl.when(sender != me)
        def _():
            remote(
                q_cut.at[0, pl.ds(0, block_rows), :], q_out.at[slot],
                q_send.at[0, 0], q_recv.at[slot], sender,
            ).wait_recv()


def output_kernel(
    n,
    hidden, attended, adapter, wo_hbm, down_hbm, up_hbm,
    result,
    buf, wo, down, up, acc, low, pieces, low_all,
    load_sem, zsend, ysend, csend, grecv, rs_send, rs_recv, lo_send, lo_recv,
):
    me = lax.axis_index("tensor")
    rows, span = hidden.shape
    block_rows, width = attended.shape
    row_blocks = rows // block_rows
    loads = [
        pltpu.make_async_copy(src, dst, load_sem.at[i])
        for i, (src, dst) in enumerate([(down_hbm, down), (wo_hbm, wo), (up_hbm, up)])
    ]
    for load in loads:
        load.start()

    def at_block(block):
        return (
            block // row_blocks,
            pl.ds(pl.multiple_of(lax.rem(block, row_blocks) * block_rows, block_rows), block_rows),
        )

    kv_group, own_rows = at_block(me)
    buf[kv_group, own_rows, :] = attended[...]
    acc[...] = hidden[...].astype(F32)
    greet_all(n, me)

    def view(block):
        group, at = at_block(block)
        return buf.at[group, at, :]

    gather = Gather(n, me, view, zsend, ysend, csend, grecv)
    gather.line(0)
    who = adapter[...]
    piece = rows // n
    reduce = Exchange(
        n, me, pieces, rs_send, rs_recv,
        lambda peer: low.at[pl.ds(pl.multiple_of(peer * piece, 8), piece), :],
    )
    spread = Exchange(n, me, low_all, lo_send, lo_recv, lambda peer: low_all.at[me])

    def first_low():
        first = pl.multiple_of(lax.rem(me, row_blocks) * span, span)
        low_partial(buf[kv_group, :, pl.ds(first, span)], down, who, low)
        pieces[me] = low[pl.ds(pl.multiple_of(me * piece, 8), piece), :]
        reduce.start()

    def second_low():
        reduce.wait_arrived()
        reduce_low(n, me, pieces, low_all)
        spread.start()

    def third_low():
        spread.wait_arrived()
        low_upward(low_all[...].reshape(rows, HEAD_SIZE), [up], who, [acc])

    early = row_blocks == 2
    for load in loads:
        load.wait()

    def step(d, carry):
        @pl.when(d + 1 < gather.depth)
        def _():
            gather.line(d + 1)

        if early:
            pl.when(d == 1)(second_low)
            pl.when(d == 2)(third_low)
        gather.rest(d)
        if early:
            pl.when(d == 0)(first_low)

        def chip_part(chip):
            block = chip * 2
            group = block // row_blocks
            first = pl.multiple_of(lax.rem(block, row_blocks) * block_rows, block_rows)
            at = pl.ds(first, 2 * block_rows)
            acc[at, :] += jnp.dot(
                buf[group, at, :], wo[pl.ds(pl.multiple_of(group * width, width), width), :],
                preferred_element_type=F32,
            )

        gather.each_chip(d, chip_part)
        return carry

    lax.fori_loop(0, gather.depth, step, 0)
    if not early:
        first_low()
        second_low()
        third_low()
    result[...] = acc[...].astype(BF16)
    reduce.wait_sent()
    spread.wait_sent()
    gather.wait_sent()


def rotate_tables(positions):
    half_width = HEAD_SIZE // 2
    frequency = rope_base ** (-(jnp.arange(half_width, dtype=F32) * 2.0) / HEAD_SIZE)
    angles = positions.astype(F32)[:, None] * frequency[None, :]
    cosine, sine = jnp.cos(angles), jnp.sin(angles)
    return (
        jnp.concatenate([cosine, cosine], axis=1),
        jnp.concatenate([-sine, sine], axis=1),
    )


def in_vmem():
    return pl.BlockSpec(memory_space=pltpu.VMEM)


def anywhere():
    return pl.BlockSpec(memory_space=pl.ANY)


def body(
    hidden,
    attention_norm_gain,
    query_weight,
    key_value_weight,
    output_weight,
    adapter_down_factors,
    adapter_query_up,
    adapter_key_value_up,
    output_adapter_down,
    output_adapter_up,
    key_cache,
    value_cache,
    adapter,
    lengths,
):
    n = lax.axis_size("tensor")
    device = lax.axis_index("tensor")
    rows, span = hidden.shape
    kv_width = key_value_weight.shape[1]
    row_blocks = n // KEY_VALUE_HEADS
    block_rows = rows // row_blocks
    slots = span // HEAD_SIZE
    dma = pltpu.SemaphoreType.DMA
    cosine, sine = rotate_tables(lengths)

    def low_table(table):
        return jnp.swapaxes(table, 1, 2).reshape(-1, table.shape[1])

    def up_table(table):
        return table.reshape(-1, table.shape[2])

    low_rows = adapter_down_factors.shape[0] * adapter_down_factors.shape[2]
    width = query_weight.shape[0]
    low_scratch = [
        pltpu.VMEM((rows, HEAD_SIZE), F32),
        pltpu.VMEM((n, rows // n, HEAD_SIZE), F32),
        pltpu.VMEM((n, rows // n, HEAD_SIZE), F32),
    ]
    queries, kv_pieces = pl.pallas_call(
        functools.partial(project_kernel, n),
        out_shape=(
            jax.ShapeDtypeStruct((GROUP_HEADS, block_rows, HEAD_SIZE), BF16),
            jax.ShapeDtypeStruct((row_blocks, block_rows, kv_width), BF16),
        ),
        in_specs=[in_vmem()] * 5 + [anywhere()] * 5,
        out_specs=(in_vmem(), in_vmem()),
        scratch_shapes=[
            pltpu.VMEM((n, rows, span), BF16),
            pltpu.VMEM((width, span), BF16),
            pltpu.VMEM((width, kv_width), BF16),
            pltpu.VMEM((low_rows, span), BF16),
            pltpu.VMEM((low_rows, span), BF16),
            pltpu.VMEM((low_rows, kv_width), BF16),
            pltpu.VMEM((rows, span), F32),
            pltpu.VMEM((rows, kv_width), F32),
            pltpu.VMEM((n, 8, rows), F32),
            pltpu.VMEM((rows, HEAD_SIZE), F32),
            pltpu.VMEM((rows, span), BF16),
        ]
        + low_scratch
        + [
            pltpu.VMEM((slots, rows, HEAD_SIZE), BF16),
            pltpu.VMEM((rows, kv_width), BF16),
            dma((5,)),
        ]
        + gather_semaphores(n)
        + [dma((n,))] * 6
        + [dma((slots, row_blocks)), dma((GROUP_HEADS,)), dma((row_blocks,)), dma((row_blocks,))],
        compiler_params=pltpu.CompilerParams(
            collective_id=0, has_side_effects=True, vmem_limit_bytes=44 << 20
        ),
        cost_estimate=pl.CostEstimate(
            flops=2 * rows * width * (span + kv_width), bytes_accessed=24 << 20, transcendentals=0
        ),
    )(
        hidden,
        attention_norm_gain.reshape(n, 1, span),
        adapter,
        cosine,
        sine,
        query_weight,
        key_value_weight,
        low_table(adapter_down_factors),
        up_table(adapter_query_up),
        up_table(adapter_key_value_up),
    )

    row_block = device % row_blocks
    first_row = row_block * block_rows
    kv_block = jnp.transpose(kv_pieces, (1, 0, 2)).reshape(block_rows, 2 * HEAD_SIZE)
    block_lengths = lax.dynamic_slice_in_dim(lengths, first_row, block_rows, 0)
    block_cosine = lax.dynamic_slice_in_dim(cosine, first_row, block_rows, 0)
    block_sine = lax.dynamic_slice_in_dim(sine, first_row, block_rows, 0)
    fresh_key = kv_block[:, :HEAD_SIZE].astype(F32)
    new_key = (
        fresh_key * block_cosine + jnp.roll(fresh_key, HEAD_SIZE // 2, axis=1) * block_sine
    ).astype(BF16)
    new_value = kv_block[:, HEAD_SIZE:]
    block_out = attend(queries, new_key, new_value, key_cache, value_cache, block_lengths)

    out_width = output_weight.shape[0]
    out_low_rows = output_adapter_down.shape[0] * output_adapter_down.shape[2]
    return pl.pallas_call(
        functools.partial(output_kernel, n),
        out_shape=jax.ShapeDtypeStruct((rows, span), BF16),
        in_specs=[in_vmem()] * 3 + [anywhere()] * 3,
        out_specs=in_vmem(),
        scratch_shapes=[
            pltpu.VMEM((KEY_VALUE_HEADS, rows, GROUP_HEADS * HEAD_SIZE), BF16),
            pltpu.VMEM((out_width, span), BF16),
            pltpu.VMEM((out_low_rows, span), BF16),
            pltpu.VMEM((out_low_rows, span), BF16),
            pltpu.VMEM((rows, span), F32),
        ]
        + low_scratch
        + [dma((3,))]
        + gather_semaphores(n)
        + [dma((n,))] * 4,
        compiler_params=pltpu.CompilerParams(
            collective_id=1, has_side_effects=True, vmem_limit_bytes=44 << 20
        ),
        cost_estimate=pl.CostEstimate(
            flops=2 * rows * out_width * span, bytes_accessed=20 << 20, transcendentals=0
        ),
    )(
        hidden,
        block_out,
        adapter,
        output_weight,
        low_table(output_adapter_down),
        up_table(output_adapter_up),
    )


def attend(queries, new_key, new_value, key_cache, value_cache, block_lengths):
    block_rows = new_key.shape[0]
    queries = jnp.transpose(queries, (1, 0, 2))
    factor = HEAD_SIZE ** (-0.5)
    scores = jnp.einsum("rgd,rpd->rgp", queries, key_cache, preferred_element_type=F32) * factor
    live = jnp.arange(key_cache.shape[1], dtype=jnp.int32)[None, :] < block_lengths[:, None]
    scores = jnp.where(live[:, None, :], scores, -jnp.inf)
    own_score = jnp.einsum("rgd,rd->rg", queries, new_key, preferred_element_type=F32) * factor
    highest = jnp.maximum(jnp.max(scores, axis=2), own_score)
    weights = jnp.exp(scores - highest[:, :, None])
    own_weight = jnp.exp(own_score - highest)
    weight_sum = jnp.sum(weights, axis=2) + own_weight
    probs = (weights / weight_sum[:, :, None]).astype(BF16)
    own_prob = (own_weight / weight_sum).astype(BF16)
    head_out = jnp.einsum("rgp,rpd->rgd", probs, value_cache, preferred_element_type=F32)
    head_out = head_out + own_prob.astype(F32)[:, :, None] * new_value.astype(F32)[:, None, :]
    return head_out.reshape(block_rows, GROUP_HEADS * HEAD_SIZE).astype(BF16)


def solution(mesh):
    placed = (
        P("groups", "tensor"),
        P(),
        P(None, "tensor"),
        P(None, "tensor"),
        P(None, "tensor"),
        P(None, "tensor", None),
        P(None, None, "tensor"),
        P(None, None, "tensor"),
        P(None, "tensor", None),
        P(None, None, "tensor"),
        P(("groups", "tensor"), None, None),
        P(("groups", "tensor"), None, None),
        P("groups", None),
        P("groups"),
    )
    return jax.shard_map(
        body, mesh=mesh, in_specs=placed, out_specs=P("groups", "tensor"), check_vma=False
    )
```

```python
import functools

import jax
import jax.numpy as jnp
from jax import lax
from jax.experimental import pallas as pl
from jax.experimental.pallas import tpu as pltpu
from jax.sharding import PartitionSpec as P

QUERY_HEADS = 64
KEY_VALUE_HEADS = 8
HEAD_SIZE = 128
GROUP_HEADS = QUERY_HEADS // KEY_VALUE_HEADS

adapter_scale = 0.5
rope_base = 500000.0
norm_eps = 1e-05

MESH = pl.DeviceIdType.MESH
F32 = jnp.float32
BF16 = jnp.bfloat16
NT = (((1,), (1,)), ((), ()))


def remote(src, dst, send_sem, recv_sem, peer):
    return pltpu.make_async_remote_copy(
        src_ref=src,
        dst_ref=dst,
        send_sem=send_sem,
        recv_sem=recv_sem,
        device_id={"tensor": peer},
        device_id_type=MESH,
    )


def greet_all(n, me):
    barrier = pltpu.get_barrier_semaphore()

    def greet(i, carry):
        pl.semaphore_signal(
            barrier, inc=1, device_id={"tensor": lax.rem(me + i, n)}, device_id_type=MESH
        )
        return carry

    lax.fori_loop(1, n, greet, 0)
    pl.semaphore_wait(barrier, n - 1)


def for_peers(n, me, action):
    def step(i, carry):
        action(i, lax.rem(me + i, n))
        return carry

    lax.fori_loop(1, n, step, 0)


class Exchange:
    def __init__(self, n, me, buf, send, recv, source):
        self.n, self.me, self.buf, self.send, self.recv, self.source = n, me, buf, send, recv, source

    def copy(self, i, peer):
        return remote(
            self.source(peer), self.buf.at[self.me], self.send.at[i], self.recv.at[self.me], peer
        )

    def start(self):
        for_peers(self.n, self.me, lambda i, peer: self.copy(i, peer).start())

    def wait_arrived(self):
        def arrived(i, peer):
            remote(
                self.source(peer), self.buf.at[peer], self.send.at[i], self.recv.at[peer], peer
            ).wait_recv()

        for_peers(self.n, self.me, arrived)

    def wait_sent(self):
        for_peers(self.n, self.me, lambda i, peer: self.copy(i, peer).wait_send())


class Gather:
    def __init__(self, n, me, view, zsend, ysend, csend, recv):
        self.wide = 2 if n % 4 == 0 and n <= 16 else 1
        self.depth = n // (2 * self.wide)
        self.view, self.me = view, me
        self.zsend, self.ysend, self.csend, self.recv = zsend, ysend, csend, recv
        self.core = lax.rem(me, 2)
        self.side = lax.rem(me // 2, self.wide)
        self.level = me // (2 * self.wide)

    def index(self, level, side, core):
        return (level * self.wide + side) * 2 + core

    def copy(self, block, send_sem, peer):
        return remote(self.view(block), self.view(block), send_sem, self.recv.at[block], peer)

    def up(self, d):
        block = self.index(self.level - d, self.side, self.core)
        return self.copy(block, self.zsend.at[0, d], self.index(self.level + 1, self.side, self.core))

    def down(self, d):
        block = self.index(self.level + d, self.side, self.core)
        return self.copy(block, self.zsend.at[1, d], self.index(self.level - 1, self.side, self.core))

    def across(self, level, sem):
        block = self.index(level, self.side, self.core)
        return self.copy(block, self.ysend.at[sem], self.index(self.level, 1 - self.side, self.core))

    def over(self, level, side, sem):
        block = self.index(level, side, self.core)
        return self.copy(
            block, self.csend.at[side, sem], self.index(self.level, self.side, 1 - self.core)
        )

    def await_block(self, block, peer):
        self.copy(block, self.zsend.at[0, 0], peer).wait_recv()

    def each_sign(self, d, action):
        @pl.when(self.level - d >= 0)
        def _():
            action(self.level - d, 0)

        @pl.when((d > 0) & (self.level + d < self.depth))
        def _():
            action(self.level + d, 1)

    def line(self, d):
        def low(level, sign):
            @pl.when(d > 0)
            def _():
                other = self.level - 1 if sign == 0 else self.level + 1
                self.await_block(
                    self.index(level, self.side, self.core),
                    self.index(other, self.side, self.core),
                )

            if sign == 0:

                @pl.when(self.level + 1 < self.depth)
                def _():
                    self.up(d).start()

                @pl.when((d == 0) & (self.level > 0))
                def _():
                    self.down(d).start()

            else:

                @pl.when(self.level > 0)
                def _():
                    self.down(d).start()

            if self.wide == 2:
                self.across(level, 2 * d + sign).start()
            self.over(level, self.side, 2 * d + sign).start()

        self.each_sign(d, low)

    def rest(self, d):
        def take(level, sign):
            if self.wide == 2:
                self.await_block(
                    self.index(level, 1 - self.side, self.core),
                    self.index(self.level, 1 - self.side, self.core),
                )
                self.over(level, 1 - self.side, 2 * d + sign).start()

        self.each_sign(d, take)

        def other(level, sign):
            for side in range(self.wide):
                self.await_block(
                    self.index(level, side, 1 - self.core),
                    self.index(self.level, self.side, 1 - self.core),
                )

        self.each_sign(d, other)

    def wait_sent(self):
        def step(d, carry):
            def sent(level, sign):
                if sign == 0:

                    @pl.when(self.level + 1 < self.depth)
                    def _():
                        self.up(d).wait_send()

                    @pl.when((d == 0) & (self.level > 0))
                    def _():
                        self.down(d).wait_send()

                else:

                    @pl.when(self.level > 0)
                    def _():
                        self.down(d).wait_send()

                if self.wide == 2:
                    self.across(level, 2 * d + sign).wait_send()
                for side in range(self.wide):
                    self.over(level, side, 2 * d + sign).wait_send()

            self.each_sign(d, sent)
            return carry

        lax.fori_loop(0, self.depth, step, 0)

    def each_chip(self, d, action):
        def step(i, carry):
            level = jnp.where(i < self.wide, self.level - d, self.level + d)
            side = lax.rem(i, self.wide)

            @pl.when((level >= 0) & (level < self.depth) & ((i < self.wide) | (d > 0)))
            def _():
                action(level * self.wide + side)

            return carry

        lax.fori_loop(0, 2 * self.wide, step, 0)


def gather_semaphores(n):
    return [
        pltpu.SemaphoreType.DMA((2, n)),
        pltpu.SemaphoreType.DMA((2 * n,)),
        pltpu.SemaphoreType.DMA((2, 2 * n)),
        pltpu.SemaphoreType.DMA((n,)),
    ]


def low_partial(values, down, adapter, low):
    rank = HEAD_SIZE // 2
    lanes = lax.broadcasted_iota(jnp.int32, (values.shape[0], HEAD_SIZE), 1) // rank
    low[...] = jnp.zeros_like(low)
    width = 4 * HEAD_SIZE

    def step(i, carry):
        spread = lax.dot_general(
            values, down[pl.ds(pl.multiple_of(i * width, width), width), :], NT,
            preferred_element_type=F32,
        )
        total = low[...]
        for part in range(width // HEAD_SIZE):
            mine = adapter == lanes + (i * (width // rank) + part * (HEAD_SIZE // rank))
            total = total + jnp.where(mine, spread[:, part * HEAD_SIZE : (part + 1) * HEAD_SIZE], 0.0)
        low[...] = total
        return carry

    lax.fori_loop(0, down.shape[0] // width, step, 0)


def low_upward(low, tables, adapter, totals):
    rank = HEAD_SIZE // 2
    lanes = lax.broadcasted_iota(jnp.int32, low.shape, 1) // rank
    width = 4 * HEAD_SIZE

    def step(i, carry):
        parts = []
        for part in range(width // HEAD_SIZE):
            mine = adapter == lanes + (i * (width // rank) + part * (HEAD_SIZE // rank))
            parts.append(jnp.where(mine, low, 0.0).astype(BF16))
        spread = jnp.concatenate(parts, axis=1)
        at = pl.ds(pl.multiple_of(i * width, width), width)
        for table, total in zip(tables, totals):
            total[...] += adapter_scale * jnp.dot(spread, table[at, :], preferred_element_type=F32)
        return carry

    lax.fori_loop(0, tables[0].shape[0] // width, step, 0)


def reduce_low(n, me, pieces, low_all):
    total = pieces[0]
    for i in range(1, n):
        total = total + pieces[i]
    total = total + pltpu.roll(total, HEAD_SIZE // 2, 1)
    low_all[me] = total.astype(BF16).astype(F32)


def project_kernel(
    n,
    hidden, gain, adapter, cosine, sine, block_cosine, block_sine, block_lengths,
    wq_hbm, wkv_hbm, down_hbm, upq_hbm, upkv_hbm, keys_hbm, values_hbm,
    block_out,
    q_out, kv_out, keys, values_ref, q_rows, new_keys, new_values, heads_out, buf, wq, wkv, down, upq, upkv, acc_q, acc_kv, stat, inv, own, low, pieces, low_all, q_cut, kv_cut,
    load_sem, zsend, ysend, csend, grecv, st_send, st_recv, rs_send, rs_recv, lo_send, lo_recv,
    q_send, q_recv, kv_send, kv_recv,
):
    me = lax.axis_index("tensor")
    rows, span = hidden.shape
    loads = [
        pltpu.make_async_copy(src, dst, load_sem.at[i])
        for i, (src, dst) in enumerate(
            [(down_hbm, down), (wq_hbm, wq), (wkv_hbm, wkv), (upq_hbm, upq), (upkv_hbm, upkv),
             (keys_hbm, keys), (values_hbm, values_ref)]
        )
    ]
    buf[me] = hidden[...]
    greet_all(n, me)
    gather = Gather(n, me, lambda block: buf.at[block], zsend, ysend, csend, grecv)
    gather.line(0)
    for load in loads:
        load.start()

    own_values = hidden[...].astype(F32)
    squares = jnp.sum(own_values * own_values, axis=1, keepdims=True)
    stat[me] = jnp.transpose(jnp.broadcast_to(squares, (rows, HEAD_SIZE)))[:8, :]
    stats = Exchange(n, me, stat, st_send, st_recv, lambda peer: stat.at[me])
    stats.start()
    acc_q[...] = jnp.zeros_like(acc_q)
    acc_kv[...] = jnp.zeros_like(acc_kv)
    stats.wait_arrived()
    total = stat[0]
    for i in range(1, n):
        total = total + stat[i]
    mean = total[0:1, :] / (n * span)
    scale = lax.rsqrt(mean + norm_eps)
    inv[...] = jnp.transpose(jnp.broadcast_to(scale, (HEAD_SIZE, rows)))

    def normed(block):
        return (
            buf[block].astype(F32) * inv[:, 0:1] * gain[block].astype(F32)
        ).astype(BF16)

    who = adapter[...]
    own[...] = normed(me)
    loads[0].wait()
    low_partial(own[...], down, who, low)
    piece = rows // n
    pieces[me] = low[pl.ds(pl.multiple_of(me * piece, 8), piece), :]
    reduce = Exchange(
        n, me, pieces, rs_send, rs_recv,
        lambda peer: low.at[pl.ds(pl.multiple_of(peer * piece, 8), piece), :],
    )
    reduce.start()
    spread = Exchange(n, me, low_all, lo_send, lo_recv, lambda peer: low_all.at[me])
    loads[1].wait()
    loads[2].wait()
    loads[3].wait()
    loads[4].wait()

    def step(d, carry):
        @pl.when(d + 1 < gather.depth)
        def _():
            gather.line(d + 1)

        @pl.when(d == 1)
        def _():
            reduce.wait_arrived()
            reduce_low(n, me, pieces, low_all)
            spread.start()

        @pl.when(d == 2)
        def _():
            spread.wait_arrived()
            low_upward(low_all[...].reshape(rows, HEAD_SIZE), [upq, upkv], who, [acc_q, acc_kv])

        gather.rest(d)

        def chip_part(chip):
            for core in range(2):
                block = chip * 2 + core
                values = normed(block)
                at = pl.ds(pl.multiple_of(block * span, span), span)
                acc_q[...] += jnp.dot(values, wq[at, :], preferred_element_type=F32)
                acc_kv[...] += jnp.dot(values, wkv[at, :], preferred_element_type=F32)

        gather.each_chip(d, chip_part)
        return carry

    lax.fori_loop(0, gather.depth, step, 0)

    row_blocks = n // KEY_VALUE_HEADS
    block_rows = rows // row_blocks
    slots = acc_q.shape[1] // HEAD_SIZE
    cos, sin = cosine[...], sine[...]
    kv_cut[...] = acc_kv[...].astype(BF16)
    kv_group = me // row_blocks

    def kv_copy(part):
        peer = kv_group * row_blocks + part
        slot = lax.rem(me, row_blocks)
        return peer, slot, remote(
            kv_cut.at[pl.ds(part * block_rows, block_rows), :], kv_out.at[slot],
            kv_send.at[part], kv_recv.at[slot], peer,
        )

    def q_copy(i, part):
        column = me * slots + i
        peer = lax.rem(column, KEY_VALUE_HEADS) * row_blocks + part
        slot = column // KEY_VALUE_HEADS
        return peer, slot, remote(
            q_cut.at[i, pl.ds(part * block_rows, block_rows), :], q_out.at[slot],
            q_send.at[i, part], q_recv.at[slot], peer,
        )

    for part in range(row_blocks):
        peer, slot, copy = kv_copy(part)

        @pl.when(peer != me)
        def _():
            copy.start()

        @pl.when(peer == me)
        def _():
            kv_out[slot] = kv_cut[pl.ds(part * block_rows, block_rows), :]

    for i in range(slots):
        values = acc_q[:, i * HEAD_SIZE : (i + 1) * HEAD_SIZE]
        q_cut[i] = (values * cos + pltpu.roll(values, HEAD_SIZE // 2, 1) * sin).astype(BF16)
        for part in range(row_blocks):
            peer, slot, copy = q_copy(i, part)

            @pl.when(peer != me)
            def _():
                copy.start()

            @pl.when(peer == me)
            def _():
                q_out[slot] = q_cut[i, pl.ds(part * block_rows, block_rows), :]

    stats.wait_sent()
    reduce.wait_sent()
    spread.wait_sent()
    gather.wait_sent()
    for part in range(row_blocks):
        peer, slot, copy = kv_copy(part)

        @pl.when(peer != me)
        def _():
            copy.wait_send()
            remote(
                kv_cut.at[pl.ds(part * block_rows, block_rows), :], kv_out.at[part],
                kv_send.at[part], kv_recv.at[part], peer,
            ).wait_recv()

    for i in range(slots):
        for part in range(row_blocks):
            peer, slot, copy = q_copy(i, part)

            @pl.when(peer != me)
            def _():
                copy.wait_send()

    for slot in range(GROUP_HEADS):
        sender = (slot * KEY_VALUE_HEADS + kv_group) // slots

        @pl.when(sender != me)
        def _():
            remote(
                q_cut.at[0, pl.ds(0, block_rows), :], q_out.at[slot],
                q_send.at[0, 0], q_recv.at[slot], sender,
            ).wait_recv()

    fresh = jnp.concatenate([kv_out[i] for i in range(row_blocks)], axis=1).astype(F32)
    fresh_key = fresh[:, :HEAD_SIZE]
    new_keys[...] = (
        fresh_key * block_cosine[...]
        + pltpu.roll(fresh_key, HEAD_SIZE // 2, 1) * block_sine[...]
    ).astype(BF16).astype(F32)
    new_values[...] = fresh[:, HEAD_SIZE:]
    for slot in range(GROUP_HEADS):
        q_rows[:, slot, :] = q_out[slot].astype(F32)
    loads[5].wait()
    loads[6].wait()
    group = 8
    cache_len = keys.shape[1]
    place = lax.broadcasted_iota(jnp.int32, (group, GROUP_HEADS, cache_len), 2)
    factor = HEAD_SIZE ** (-0.5)

    def some_rows(i, carry):
        at = pl.ds(pl.multiple_of(i * group, group), group)
        queries = q_rows[at]
        scores = factor * lax.dot_general(
            queries.astype(BF16), keys[at], (((2,), (2,)), ((0,), (0,))),
            preferred_element_type=F32,
        )
        scores = jnp.where(place < block_lengths[at], scores, -jnp.inf)
        own_score = factor * jnp.sum(queries * new_keys[at][:, None, :], axis=2, keepdims=True)
        highest = jnp.maximum(jnp.max(scores, axis=2, keepdims=True), own_score)
        weights = jnp.exp(scores - highest)
        own_weight = jnp.exp(own_score - highest)
        share = 1.0 / (jnp.sum(weights, axis=2, keepdims=True) + own_weight)
        heads = lax.dot_general(
            (weights * share).astype(BF16), values_ref[at], (((2,), (1,)), ((0,), (0,))),
            preferred_element_type=F32,
        )
        own_prob = (own_weight * share).astype(BF16).astype(F32)
        heads_out[at] = heads + own_prob * new_values[at][:, None, :]
        return carry

    lax.fori_loop(0, block_rows // group, some_rows, 0)
    for slot in range(GROUP_HEADS):
        block_out[:, slot * HEAD_SIZE : (slot + 1) * HEAD_SIZE] = heads_out[:, slot, :].astype(BF16)


def output_kernel(
    n,
    hidden, attended, adapter, wo_hbm, down_hbm, up_hbm,
    result,
    buf, wo, down, up, acc, low, pieces, low_all,
    load_sem, zsend, ysend, csend, grecv, rs_send, rs_recv, lo_send, lo_recv,
):
    me = lax.axis_index("tensor")
    rows, span = hidden.shape
    block_rows, width = attended.shape
    row_blocks = rows // block_rows
    loads = [
        pltpu.make_async_copy(src, dst, load_sem.at[i])
        for i, (src, dst) in enumerate([(down_hbm, down), (wo_hbm, wo), (up_hbm, up)])
    ]
    for load in loads:
        load.start()

    def at_block(block):
        return (
            block // row_blocks,
            pl.ds(pl.multiple_of(lax.rem(block, row_blocks) * block_rows, block_rows), block_rows),
        )

    kv_group, own_rows = at_block(me)
    buf[kv_group, own_rows, :] = attended[...]
    acc[...] = hidden[...].astype(F32)
    greet_all(n, me)

    def view(block):
        group, at = at_block(block)
        return buf.at[group, at, :]

    gather = Gather(n, me, view, zsend, ysend, csend, grecv)
    gather.line(0)
    who = adapter[...]
    piece = rows // n
    reduce = Exchange(
        n, me, pieces, rs_send, rs_recv,
        lambda peer: low.at[pl.ds(pl.multiple_of(peer * piece, 8), piece), :],
    )
    spread = Exchange(n, me, low_all, lo_send, lo_recv, lambda peer: low_all.at[me])

    def first_low():
        first = pl.multiple_of(lax.rem(me, row_blocks) * span, span)
        low_partial(buf[kv_group, :, pl.ds(first, span)], down, who, low)
        pieces[me] = low[pl.ds(pl.multiple_of(me * piece, 8), piece), :]
        reduce.start()

    def second_low():
        reduce.wait_arrived()
        reduce_low(n, me, pieces, low_all)
        spread.start()

    def third_low():
        spread.wait_arrived()
        low_upward(low_all[...].reshape(rows, HEAD_SIZE), [up], who, [acc])

    early = row_blocks == 2
    for load in loads:
        load.wait()

    def step(d, carry):
        @pl.when(d + 1 < gather.depth)
        def _():
            gather.line(d + 1)

        if early:
            pl.when(d == 1)(second_low)
            pl.when(d == 2)(third_low)
        gather.rest(d)
        if early:
            pl.when(d == 0)(first_low)

        def chip_part(chip):
            block = chip * 2
            group = block // row_blocks
            first = pl.multiple_of(lax.rem(block, row_blocks) * block_rows, block_rows)
            at = pl.ds(first, 2 * block_rows)
            acc[at, :] += jnp.dot(
                buf[group, at, :], wo[pl.ds(pl.multiple_of(group * width, width), width), :],
                preferred_element_type=F32,
            )

        gather.each_chip(d, chip_part)
        return carry

    lax.fori_loop(0, gather.depth, step, 0)
    if not early:
        first_low()
        second_low()
        third_low()
    result[...] = acc[...].astype(BF16)
    reduce.wait_sent()
    spread.wait_sent()
    gather.wait_sent()


def rotate_tables(positions):
    half_width = HEAD_SIZE // 2
    frequency = rope_base ** (-(jnp.arange(half_width, dtype=F32) * 2.0) / HEAD_SIZE)
    angles = positions.astype(F32)[:, None] * frequency[None, :]
    cosine, sine = jnp.cos(angles), jnp.sin(angles)
    return (
        jnp.concatenate([cosine, cosine], axis=1),
        jnp.concatenate([-sine, sine], axis=1),
    )


def in_vmem():
    return pl.BlockSpec(memory_space=pltpu.VMEM)


def anywhere():
    return pl.BlockSpec(memory_space=pl.ANY)


def body(
    hidden,
    attention_norm_gain,
    query_weight,
    key_value_weight,
    output_weight,
    adapter_down_factors,
    adapter_query_up,
    adapter_key_value_up,
    output_adapter_down,
    output_adapter_up,
    key_cache,
    value_cache,
    adapter,
    lengths,
):
    n = lax.axis_size("tensor")
    device = lax.axis_index("tensor")
    rows, span = hidden.shape
    kv_width = key_value_weight.shape[1]
    row_blocks = n // KEY_VALUE_HEADS
    block_rows = rows // row_blocks
    slots = span // HEAD_SIZE
    dma = pltpu.SemaphoreType.DMA
    cosine, sine = rotate_tables(lengths)

    def low_table(table):
        return jnp.swapaxes(table, 1, 2).reshape(-1, table.shape[1])

    def up_table(table):
        return table.reshape(-1, table.shape[2])

    low_rows = adapter_down_factors.shape[0] * adapter_down_factors.shape[2]
    width = query_weight.shape[0]
    low_scratch = [
        pltpu.VMEM((rows, HEAD_SIZE), F32),
        pltpu.VMEM((n, rows // n, HEAD_SIZE), F32),
        pltpu.VMEM((n, rows // n, HEAD_SIZE), F32),
    ]
    first_row = (device % row_blocks) * block_rows
    block_lengths = lax.dynamic_slice_in_dim(lengths, first_row, block_rows, 0)
    block_cosine, block_sine = rotate_tables(block_lengths)
    block_out = pl.pallas_call(
        functools.partial(project_kernel, n),
        out_shape=jax.ShapeDtypeStruct((block_rows, GROUP_HEADS * HEAD_SIZE), BF16),
        in_specs=[in_vmem()] * 8 + [anywhere()] * 7,
        out_specs=in_vmem(),
        scratch_shapes=[
            pltpu.VMEM((GROUP_HEADS, block_rows, HEAD_SIZE), BF16),
            pltpu.VMEM((row_blocks, block_rows, kv_width), BF16),
            pltpu.VMEM(key_cache.shape, BF16),
            pltpu.VMEM(value_cache.shape, BF16),
            pltpu.VMEM((block_rows, GROUP_HEADS, HEAD_SIZE), F32),
            pltpu.VMEM((block_rows, HEAD_SIZE), F32),
            pltpu.VMEM((block_rows, HEAD_SIZE), F32),
            pltpu.VMEM((block_rows, GROUP_HEADS, HEAD_SIZE), F32),
            pltpu.VMEM((n, rows, span), BF16),
            pltpu.VMEM((width, span), BF16),
            pltpu.VMEM((width, kv_width), BF16),
            pltpu.VMEM((low_rows, span), BF16),
            pltpu.VMEM((low_rows, span), BF16),
            pltpu.VMEM((low_rows, kv_width), BF16),
            pltpu.VMEM((rows, span), F32),
            pltpu.VMEM((rows, kv_width), F32),
            pltpu.VMEM((n, 8, rows), F32),
            pltpu.VMEM((rows, HEAD_SIZE), F32),
            pltpu.VMEM((rows, span), BF16),
        ]
        + low_scratch
        + [
            pltpu.VMEM((slots, rows, HEAD_SIZE), BF16),
            pltpu.VMEM((rows, kv_width), BF16),
            dma((7,)),
        ]
        + gather_semaphores(n)
        + [dma((n,))] * 6
        + [dma((slots, row_blocks)), dma((GROUP_HEADS,)), dma((row_blocks,)), dma((row_blocks,))],
        compiler_params=pltpu.CompilerParams(
            collective_id=0, has_side_effects=True, vmem_limit_bytes=63 << 20
        ),
        cost_estimate=pl.CostEstimate(
            flops=2 * rows * width * (span + kv_width), bytes_accessed=24 << 20, transcendentals=0
        ),
    )(
        hidden,
        attention_norm_gain.reshape(n, 1, span),
        adapter,
        cosine,
        sine,
        block_cosine,
        block_sine,
        block_lengths.reshape(block_rows, 1, 1),
        query_weight,
        key_value_weight,
        low_table(adapter_down_factors),
        up_table(adapter_query_up),
        up_table(adapter_key_value_up),
        key_cache,
        value_cache,
    )

    out_width = output_weight.shape[0]
    out_low_rows = output_adapter_down.shape[0] * output_adapter_down.shape[2]
    return pl.pallas_call(
        functools.partial(output_kernel, n),
        out_shape=jax.ShapeDtypeStruct((rows, span), BF16),
        in_specs=[in_vmem()] * 3 + [anywhere()] * 3,
        out_specs=in_vmem(),
        scratch_shapes=[
            pltpu.VMEM((KEY_VALUE_HEADS, rows, GROUP_HEADS * HEAD_SIZE), BF16),
            pltpu.VMEM((out_width, span), BF16),
            pltpu.VMEM((out_low_rows, span), BF16),
            pltpu.VMEM((out_low_rows, span), BF16),
            pltpu.VMEM((rows, span), F32),
        ]
        + low_scratch
        + [dma((3,))]
        + gather_semaphores(n)
        + [dma((n,))] * 4,
        compiler_params=pltpu.CompilerParams(
            collective_id=1, has_side_effects=True, vmem_limit_bytes=60 << 20
        ),
        cost_estimate=pl.CostEstimate(
            flops=2 * rows * out_width * span, bytes_accessed=20 << 20, transcendentals=0
        ),
    )(
        hidden,
        block_out,
        adapter,
        output_weight,
        low_table(output_adapter_down),
        up_table(output_adapter_up),
    )


def solution(mesh):
    placed = (
        P("groups", "tensor"),
        P(),
        P(None, "tensor"),
        P(None, "tensor"),
        P(None, "tensor"),
        P(None, "tensor", None),
        P(None, None, "tensor"),
        P(None, None, "tensor"),
        P(None, "tensor", None),
        P(None, None, "tensor"),
        P(("groups", "tensor"), None, None),
        P(("groups", "tensor"), None, None),
        P("groups", None),
        P("groups"),
    )
    return jax.shard_map(
        body, mesh=mesh, in_specs=placed, out_specs=P("groups", "tensor"), check_vma=False
    )
```

```python
import functools

import jax
import jax.numpy as jnp
from jax import lax
from jax.experimental import pallas as pl
from jax.experimental.pallas import tpu as pltpu
from jax.sharding import PartitionSpec as P

QUERY_HEADS = 64
KEY_VALUE_HEADS = 8
HEAD_SIZE = 128
GROUP_HEADS = QUERY_HEADS // KEY_VALUE_HEADS

adapter_scale = 0.5
rope_base = 500000.0
norm_eps = 1e-05

MESH = pl.DeviceIdType.MESH
F32 = jnp.float32
BF16 = jnp.bfloat16
NT = (((1,), (1,)), ((), ()))


def remote(src, dst, send_sem, recv_sem, peer):
    return pltpu.make_async_remote_copy(
        src_ref=src,
        dst_ref=dst,
        send_sem=send_sem,
        recv_sem=recv_sem,
        device_id={"tensor": peer},
        device_id_type=MESH,
    )


def greet_all(n, me):
    barrier = pltpu.get_barrier_semaphore()

    def greet(i, carry):
        pl.semaphore_signal(
            barrier, inc=1, device_id={"tensor": lax.rem(me + i, n)}, device_id_type=MESH
        )
        return carry

    lax.fori_loop(1, n, greet, 0)
    pl.semaphore_wait(barrier, n - 1)


def for_peers(n, me, action):
    def step(i, carry):
        action(i, lax.rem(me + i, n))
        return carry

    lax.fori_loop(1, n, step, 0)


class Exchange:
    def __init__(self, n, me, buf, send, recv, source):
        self.n, self.me, self.buf, self.send, self.recv, self.source = n, me, buf, send, recv, source

    def copy(self, i, peer):
        return remote(
            self.source(peer), self.buf.at[self.me], self.send.at[i], self.recv.at[self.me], peer
        )

    def start(self):
        for_peers(self.n, self.me, lambda i, peer: self.copy(i, peer).start())

    def wait_arrived(self):
        def arrived(i, peer):
            remote(
                self.source(peer), self.buf.at[peer], self.send.at[i], self.recv.at[peer], peer
            ).wait_recv()

        for_peers(self.n, self.me, arrived)

    def wait_sent(self):
        for_peers(self.n, self.me, lambda i, peer: self.copy(i, peer).wait_send())


class Gather:
    def __init__(self, n, me, view, zsend, ysend, csend, recv):
        self.wide = 2 if n % 4 == 0 and n <= 16 else 1
        self.depth = n // (2 * self.wide)
        self.view, self.me = view, me
        self.zsend, self.ysend, self.csend, self.recv = zsend, ysend, csend, recv
        self.core = lax.rem(me, 2)
        self.side = lax.rem(me // 2, self.wide)
        self.level = me // (2 * self.wide)

    def index(self, level, side, core):
        return (level * self.wide + side) * 2 + core

    def copy(self, block, send_sem, peer):
        return remote(self.view(block), self.view(block), send_sem, self.recv.at[block], peer)

    def up(self, d):
        block = self.index(self.level - d, self.side, self.core)
        return self.copy(block, self.zsend.at[0, d], self.index(self.level + 1, self.side, self.core))

    def down(self, d):
        block = self.index(self.level + d, self.side, self.core)
        return self.copy(block, self.zsend.at[1, d], self.index(self.level - 1, self.side, self.core))

    def across(self, level, sem):
        block = self.index(level, self.side, self.core)
        return self.copy(block, self.ysend.at[sem], self.index(self.level, 1 - self.side, self.core))

    def over(self, level, side, sem):
        block = self.index(level, side, self.core)
        return self.copy(
            block, self.csend.at[side, sem], self.index(self.level, self.side, 1 - self.core)
        )

    def await_block(self, block, peer):
        self.copy(block, self.zsend.at[0, 0], peer).wait_recv()

    def each_sign(self, d, action):
        @pl.when(self.level - d >= 0)
        def _():
            action(self.level - d, 0)

        @pl.when((d > 0) & (self.level + d < self.depth))
        def _():
            action(self.level + d, 1)

    def line(self, d):
        def low(level, sign):
            @pl.when(d > 0)
            def _():
                other = self.level - 1 if sign == 0 else self.level + 1
                self.await_block(
                    self.index(level, self.side, self.core),
                    self.index(other, self.side, self.core),
                )

            if sign == 0:

                @pl.when(self.level + 1 < self.depth)
                def _():
                    self.up(d).start()

                @pl.when((d == 0) & (self.level > 0))
                def _():
                    self.down(d).start()

            else:

                @pl.when(self.level > 0)
                def _():
                    self.down(d).start()

            if self.wide == 2:
                self.across(level, 2 * d + sign).start()
            self.over(level, self.side, 2 * d + sign).start()

        self.each_sign(d, low)

    def rest(self, d):
        def take(level, sign):
            if self.wide == 2:
                self.await_block(
                    self.index(level, 1 - self.side, self.core),
                    self.index(self.level, 1 - self.side, self.core),
                )
                self.over(level, 1 - self.side, 2 * d + sign).start()

        self.each_sign(d, take)

        def other(level, sign):
            for side in range(self.wide):
                self.await_block(
                    self.index(level, side, 1 - self.core),
                    self.index(self.level, self.side, 1 - self.core),
                )

        self.each_sign(d, other)

    def wait_sent(self):
        def step(d, carry):
            def sent(level, sign):
                if sign == 0:

                    @pl.when(self.level + 1 < self.depth)
                    def _():
                        self.up(d).wait_send()

                    @pl.when((d == 0) & (self.level > 0))
                    def _():
                        self.down(d).wait_send()

                else:

                    @pl.when(self.level > 0)
                    def _():
                        self.down(d).wait_send()

                if self.wide == 2:
                    self.across(level, 2 * d + sign).wait_send()
                for side in range(self.wide):
                    self.over(level, side, 2 * d + sign).wait_send()

            self.each_sign(d, sent)
            return carry

        lax.fori_loop(0, self.depth, step, 0)

    def each_chip(self, d, action):
        def step(i, carry):
            level = jnp.where(i < self.wide, self.level - d, self.level + d)
            side = lax.rem(i, self.wide)

            @pl.when((level >= 0) & (level < self.depth) & ((i < self.wide) | (d > 0)))
            def _():
                action(level * self.wide + side)

            return carry

        lax.fori_loop(0, 2 * self.wide, step, 0)


def gather_semaphores(n):
    return [
        pltpu.SemaphoreType.DMA((2, n)),
        pltpu.SemaphoreType.DMA((2 * n,)),
        pltpu.SemaphoreType.DMA((2, 2 * n)),
        pltpu.SemaphoreType.DMA((n,)),
    ]


def low_partial(values, down, adapter, low):
    rank = HEAD_SIZE // 2
    lanes = lax.broadcasted_iota(jnp.int32, (values.shape[0], HEAD_SIZE), 1) // rank
    low[...] = jnp.zeros_like(low)
    width = 4 * HEAD_SIZE

    def step(i, carry):
        spread = lax.dot_general(
            values, down[pl.ds(pl.multiple_of(i * width, width), width), :], NT,
            preferred_element_type=F32,
        )
        total = low[...]
        for part in range(width // HEAD_SIZE):
            mine = adapter == lanes + (i * (width // rank) + part * (HEAD_SIZE // rank))
            total = total + jnp.where(mine, spread[:, part * HEAD_SIZE : (part + 1) * HEAD_SIZE], 0.0)
        low[...] = total
        return carry

    lax.fori_loop(0, down.shape[0] // width, step, 0)


def low_upward(low, tables, adapter, totals):
    rank = HEAD_SIZE // 2
    lanes = lax.broadcasted_iota(jnp.int32, low.shape, 1) // rank
    width = 4 * HEAD_SIZE

    def step(i, carry):
        parts = []
        for part in range(width // HEAD_SIZE):
            mine = adapter == lanes + (i * (width // rank) + part * (HEAD_SIZE // rank))
            parts.append(jnp.where(mine, low, 0.0).astype(BF16))
        spread = jnp.concatenate(parts, axis=1)
        at = pl.ds(pl.multiple_of(i * width, width), width)
        for table, total in zip(tables, totals):
            total[...] += adapter_scale * jnp.dot(spread, table[at, :], preferred_element_type=F32)
        return carry

    lax.fori_loop(0, tables[0].shape[0] // width, step, 0)


def reduce_low(n, me, pieces, low_all):
    total = pieces[0]
    for i in range(1, n):
        total = total + pieces[i]
    total = total + pltpu.roll(total, HEAD_SIZE // 2, 1)
    low_all[me] = total.astype(BF16).astype(F32)


def project_kernel(
    n,
    hidden, gain, adapter, cosine, sine, lengths,
    wq_hbm, wkv_hbm, down_hbm, upq_hbm, upkv_hbm, keys_hbm, values_hbm,
    block_out,
    q_out, kv_out, keys, values_ref, q_rows, new_keys, new_values, heads_out, buf, wq, wkv, down, upq, upkv, acc_q, acc_kv, stat, inv, own, low, pieces, low_all, q_cut, kv_cut,
    load_sem, zsend, ysend, csend, grecv, st_send, st_recv, rs_send, rs_recv, lo_send, lo_recv,
    q_send, q_recv, kv_send, kv_recv,
):
    me = lax.axis_index("tensor")
    rows, span = hidden.shape
    loads = [
        pltpu.make_async_copy(src, dst, load_sem.at[i])
        for i, (src, dst) in enumerate(
            [(down_hbm, down), (wq_hbm, wq), (wkv_hbm, wkv), (upq_hbm, upq), (upkv_hbm, upkv),
             (keys_hbm, keys), (values_hbm, values_ref)]
        )
    ]
    for load in loads[:5]:
        load.start()
    buf[me] = hidden[...]
    greet_all(n, me)
    gather = Gather(n, me, lambda block: buf.at[block], zsend, ysend, csend, grecv)
    gather.line(0)

    own_values = hidden[...].astype(F32)
    squares = jnp.sum(own_values * own_values, axis=1, keepdims=True)
    stat[me] = jnp.transpose(jnp.broadcast_to(squares, (rows, HEAD_SIZE)))[:8, :]
    stats = Exchange(n, me, stat, st_send, st_recv, lambda peer: stat.at[me])
    stats.start()
    acc_q[...] = jnp.zeros_like(acc_q)
    acc_kv[...] = jnp.zeros_like(acc_kv)
    stats.wait_arrived()
    total = stat[0]
    for i in range(1, n):
        total = total + stat[i]
    mean = total[0:1, :] / (n * span)
    scale = lax.rsqrt(mean + norm_eps)
    inv[...] = jnp.transpose(jnp.broadcast_to(scale, (HEAD_SIZE, rows)))

    def normed(block):
        return (
            buf[block].astype(F32) * inv[:, 0:1] * gain[:, pl.ds(pl.multiple_of(block * span, span), span)].astype(F32)
        ).astype(BF16)

    who = adapter[...]
    own[...] = normed(me)
    loads[0].wait()
    low_partial(own[...], down, who, low)
    piece = rows // n
    pieces[me] = low[pl.ds(pl.multiple_of(me * piece, 8), piece), :]
    reduce = Exchange(
        n, me, pieces, rs_send, rs_recv,
        lambda peer: low.at[pl.ds(pl.multiple_of(peer * piece, 8), piece), :],
    )
    reduce.start()
    spread = Exchange(n, me, low_all, lo_send, lo_recv, lambda peer: low_all.at[me])
    def step(d, carry):
        @pl.when(d + 1 < gather.depth)
        def _():
            gather.line(d + 1)

        @pl.when(d == 1)
        def _():
            reduce.wait_arrived()
            reduce_low(n, me, pieces, low_all)
            spread.start()

        @pl.when(d == 2)
        def _():
            spread.wait_arrived()
            low_upward(low_all[...].reshape(rows, HEAD_SIZE), [upq, upkv], who, [acc_q, acc_kv])

        gather.rest(d)

        @pl.when(d == 0)
        def _():
            for load in loads[1:5]:
                load.wait()
            for load in loads[5:]:
                load.start()

        def chip_part(chip):
            for core in range(2):
                block = chip * 2 + core
                values = normed(block)
                at = pl.ds(pl.multiple_of(block * span, span), span)
                acc_q[...] += jnp.dot(values, wq[at, :], preferred_element_type=F32)
                acc_kv[...] += jnp.dot(values, wkv[at, :], preferred_element_type=F32)

        gather.each_chip(d, chip_part)
        return carry

    lax.fori_loop(0, gather.depth, step, 0)

    row_blocks = n // KEY_VALUE_HEADS
    block_rows = rows // row_blocks
    slots = acc_q.shape[1] // HEAD_SIZE
    cos, sin = cosine[...], sine[...]
    kv_cut[...] = acc_kv[...].astype(BF16)
    kv_group = me // row_blocks

    def kv_copy(part):
        peer = kv_group * row_blocks + part
        slot = lax.rem(me, row_blocks)
        return peer, slot, remote(
            kv_cut.at[pl.ds(part * block_rows, block_rows), :], kv_out.at[slot],
            kv_send.at[part], kv_recv.at[slot], peer,
        )

    def q_copy(i, part):
        column = me * slots + i
        peer = lax.rem(column, KEY_VALUE_HEADS) * row_blocks + part
        slot = column // KEY_VALUE_HEADS
        return peer, slot, remote(
            q_cut.at[i, pl.ds(part * block_rows, block_rows), :], q_out.at[slot],
            q_send.at[i, part], q_recv.at[slot], peer,
        )

    for part in range(row_blocks):
        peer, slot, copy = kv_copy(part)

        @pl.when(peer != me)
        def _():
            copy.start()

        @pl.when(peer == me)
        def _():
            kv_out[slot] = kv_cut[pl.ds(part * block_rows, block_rows), :]

    for i in range(slots):
        values = acc_q[:, i * HEAD_SIZE : (i + 1) * HEAD_SIZE]
        q_cut[i] = (values * cos + pltpu.roll(values, HEAD_SIZE // 2, 1) * sin).astype(BF16)
        for part in range(row_blocks):
            peer, slot, copy = q_copy(i, part)

            @pl.when(peer != me)
            def _():
                copy.start()

            @pl.when(peer == me)
            def _():
                q_out[slot] = q_cut[i, pl.ds(part * block_rows, block_rows), :]

    stats.wait_sent()
    reduce.wait_sent()
    spread.wait_sent()
    gather.wait_sent()
    for part in range(row_blocks):
        peer, slot, copy = kv_copy(part)

        @pl.when(peer != me)
        def _():
            copy.wait_send()
            remote(
                kv_cut.at[pl.ds(part * block_rows, block_rows), :], kv_out.at[part],
                kv_send.at[part], kv_recv.at[part], peer,
            ).wait_recv()

    for i in range(slots):
        for part in range(row_blocks):
            peer, slot, copy = q_copy(i, part)

            @pl.when(peer != me)
            def _():
                copy.wait_send()

    for slot in range(GROUP_HEADS):
        sender = (slot * KEY_VALUE_HEADS + kv_group) // slots

        @pl.when(sender != me)
        def _():
            remote(
                q_cut.at[0, pl.ds(0, block_rows), :], q_out.at[slot],
                q_send.at[0, 0], q_recv.at[slot], sender,
            ).wait_recv()

    first_row = lax.rem(me, row_blocks) * block_rows
    block_at = pl.ds(pl.multiple_of(first_row, block_rows), block_rows)
    fresh = jnp.concatenate([kv_out[i] for i in range(row_blocks)], axis=1).astype(F32)
    fresh_key = fresh[:, :HEAD_SIZE]
    new_keys[...] = (
        fresh_key * cosine[block_at, :]
        + pltpu.roll(fresh_key, HEAD_SIZE // 2, 1) * sine[block_at, :]
    ).astype(BF16).astype(F32)
    new_values[...] = fresh[:, HEAD_SIZE:]
    for slot in range(GROUP_HEADS):
        q_rows[:, slot, :] = q_out[slot].astype(F32)
    loads[5].wait()
    loads[6].wait()
    group = 16
    cache_len = keys.shape[1]
    place = lax.broadcasted_iota(jnp.int32, (group, GROUP_HEADS, cache_len), 2)
    factor = HEAD_SIZE ** (-0.5)

    def some_rows(i, carry):
        at = pl.ds(pl.multiple_of(i * group, group), group)
        queries = q_rows[at]
        scores = factor * lax.dot_general(
            queries.astype(BF16), keys[at], (((2,), (2,)), ((0,), (0,))),
            preferred_element_type=F32,
        )
        scores = jnp.where(place < lengths[pl.ds(first_row + i * group, group)], scores, -jnp.inf)
        own_score = factor * jnp.sum(queries * new_keys[at][:, None, :], axis=2, keepdims=True)
        highest = jnp.maximum(jnp.max(scores, axis=2, keepdims=True), own_score)
        weights = jnp.exp(scores - highest)
        own_weight = jnp.exp(own_score - highest)
        share = 1.0 / (jnp.sum(weights, axis=2, keepdims=True) + own_weight)
        heads = lax.dot_general(
            (weights * share).astype(BF16), values_ref[at], (((2,), (1,)), ((0,), (0,))),
            preferred_element_type=F32,
        )
        own_prob = (own_weight * share).astype(BF16).astype(F32)
        heads_out[at] = heads + own_prob * new_values[at][:, None, :]
        return carry

    lax.fori_loop(0, block_rows // group, some_rows, 0)
    for slot in range(GROUP_HEADS):
        block_out[:, slot * HEAD_SIZE : (slot + 1) * HEAD_SIZE] = heads_out[:, slot, :].astype(BF16)


def output_kernel(
    n,
    hidden, attended, adapter, wo_hbm, down_hbm, up_hbm,
    result,
    buf, wo, down, up, acc, low, pieces, low_all,
    load_sem, zsend, ysend, csend, grecv, rs_send, rs_recv, lo_send, lo_recv,
):
    me = lax.axis_index("tensor")
    rows, span = hidden.shape
    block_rows, width = attended.shape
    row_blocks = rows // block_rows
    loads = [
        pltpu.make_async_copy(src, dst, load_sem.at[i])
        for i, (src, dst) in enumerate([(down_hbm, down), (wo_hbm, wo), (up_hbm, up)])
    ]
    for load in loads:
        load.start()

    def at_block(block):
        return (
            block // row_blocks,
            pl.ds(pl.multiple_of(lax.rem(block, row_blocks) * block_rows, block_rows), block_rows),
        )

    kv_group, own_rows = at_block(me)
    buf[kv_group, own_rows, :] = attended[...]
    acc[...] = hidden[...].astype(F32)
    greet_all(n, me)

    def view(block):
        group, at = at_block(block)
        return buf.at[group, at, :]

    gather = Gather(n, me, view, zsend, ysend, csend, grecv)
    gather.line(0)
    who = adapter[...]
    piece = rows // n
    reduce = Exchange(
        n, me, pieces, rs_send, rs_recv,
        lambda peer: low.at[pl.ds(pl.multiple_of(peer * piece, 8), piece), :],
    )
    spread = Exchange(n, me, low_all, lo_send, lo_recv, lambda peer: low_all.at[me])

    def first_low():
        first = pl.multiple_of(lax.rem(me, row_blocks) * span, span)
        low_partial(buf[kv_group, :, pl.ds(first, span)], down, who, low)
        pieces[me] = low[pl.ds(pl.multiple_of(me * piece, 8), piece), :]
        reduce.start()

    def second_low():
        reduce.wait_arrived()
        reduce_low(n, me, pieces, low_all)
        spread.start()

    def third_low():
        spread.wait_arrived()
        low_upward(low_all[...].reshape(rows, HEAD_SIZE), [up], who, [acc])

    early = row_blocks == 2

    def step(d, carry):
        @pl.when(d + 1 < gather.depth)
        def _():
            gather.line(d + 1)

        if early:
            pl.when(d == 1)(second_low)
            pl.when(d == 2)(third_low)
        gather.rest(d)

        @pl.when(d == 0)
        def _():
            for load in loads:
                load.wait()

        if early:
            pl.when(d == 0)(first_low)

        def chip_part(chip):
            block = chip * 2
            group = block // row_blocks
            first = pl.multiple_of(lax.rem(block, row_blocks) * block_rows, block_rows)
            at = pl.ds(first, 2 * block_rows)
            acc[at, :] += jnp.dot(
                buf[group, at, :], wo[pl.ds(pl.multiple_of(group * width, width), width), :],
                preferred_element_type=F32,
            )

        gather.each_chip(d, chip_part)
        return carry

    lax.fori_loop(0, gather.depth, step, 0)
    if not early:
        first_low()
        second_low()
        third_low()
    result[...] = acc[...].astype(BF16)
    reduce.wait_sent()
    spread.wait_sent()
    gather.wait_sent()


def rotate_tables(positions):
    half_width = HEAD_SIZE // 2
    entry = jnp.arange(HEAD_SIZE, dtype=jnp.int32)
    frequency = rope_base ** (-((entry % half_width).astype(F32) * 2.0) / HEAD_SIZE)
    angles = positions.astype(F32)[:, None] * frequency[None, :]
    sign = jnp.where(entry < half_width, -1.0, 1.0).astype(F32)
    return jnp.cos(angles), jnp.sin(angles) * sign[None, :]


def in_vmem():
    return pl.BlockSpec(memory_space=pltpu.VMEM)


def anywhere():
    return pl.BlockSpec(memory_space=pl.ANY)


def body(
    hidden,
    attention_norm_gain,
    query_weight,
    key_value_weight,
    output_weight,
    adapter_down_factors,
    adapter_query_up,
    adapter_key_value_up,
    output_adapter_down,
    output_adapter_up,
    key_cache,
    value_cache,
    adapter,
    lengths,
):
    n = lax.axis_size("tensor")
    rows, span = hidden.shape
    kv_width = key_value_weight.shape[1]
    row_blocks = n // KEY_VALUE_HEADS
    block_rows = rows // row_blocks
    slots = span // HEAD_SIZE
    dma = pltpu.SemaphoreType.DMA
    cosine, sine = rotate_tables(lengths)

    def low_table(table):
        return jnp.swapaxes(table, 1, 2).reshape(-1, table.shape[1])

    def up_table(table):
        return table.reshape(-1, table.shape[2])

    low_rows = adapter_down_factors.shape[0] * adapter_down_factors.shape[2]
    width = query_weight.shape[0]
    low_scratch = [
        pltpu.VMEM((rows, HEAD_SIZE), F32),
        pltpu.VMEM((n, rows // n, HEAD_SIZE), F32),
        pltpu.VMEM((n, rows // n, HEAD_SIZE), F32),
    ]
    block_out = pl.pallas_call(
        functools.partial(project_kernel, n),
        out_shape=jax.ShapeDtypeStruct((block_rows, GROUP_HEADS * HEAD_SIZE), BF16),
        in_specs=[in_vmem()] * 6 + [anywhere()] * 7,
        out_specs=in_vmem(),
        scratch_shapes=[
            pltpu.VMEM((GROUP_HEADS, block_rows, HEAD_SIZE), BF16),
            pltpu.VMEM((row_blocks, block_rows, kv_width), BF16),
            pltpu.VMEM(key_cache.shape, BF16),
            pltpu.VMEM(value_cache.shape, BF16),
            pltpu.VMEM((block_rows, GROUP_HEADS, HEAD_SIZE), F32),
            pltpu.VMEM((block_rows, HEAD_SIZE), F32),
            pltpu.VMEM((block_rows, HEAD_SIZE), F32),
            pltpu.VMEM((block_rows, GROUP_HEADS, HEAD_SIZE), F32),
            pltpu.VMEM((n, rows, span), BF16),
            pltpu.VMEM((width, span), BF16),
            pltpu.VMEM((width, kv_width), BF16),
            pltpu.VMEM((low_rows, span), BF16),
            pltpu.VMEM((low_rows, span), BF16),
            pltpu.VMEM((low_rows, kv_width), BF16),
            pltpu.VMEM((rows, span), F32),
            pltpu.VMEM((rows, kv_width), F32),
            pltpu.VMEM((n, 8, rows), F32),
            pltpu.VMEM((rows, HEAD_SIZE), F32),
            pltpu.VMEM((rows, span), BF16),
        ]
        + low_scratch
        + [
            pltpu.VMEM((slots, rows, HEAD_SIZE), BF16),
            pltpu.VMEM((rows, kv_width), BF16),
            dma((7,)),
        ]
        + gather_semaphores(n)
        + [dma((n,))] * 6
        + [dma((slots, row_blocks)), dma((GROUP_HEADS,)), dma((row_blocks,)), dma((row_blocks,))],
        compiler_params=pltpu.CompilerParams(
            collective_id=0, has_side_effects=True, vmem_limit_bytes=63 << 20
        ),
        cost_estimate=pl.CostEstimate(
            flops=2 * rows * width * (span + kv_width), bytes_accessed=24 << 20, transcendentals=0
        ),
    )(
        hidden,
        attention_norm_gain.reshape(1, n * span),
        adapter,
        cosine,
        sine,
        lengths.reshape(rows, 1, 1),
        query_weight,
        key_value_weight,
        low_table(adapter_down_factors),
        up_table(adapter_query_up),
        up_table(adapter_key_value_up),
        key_cache,
        value_cache,
    )

    out_width = output_weight.shape[0]
    out_low_rows = output_adapter_down.shape[0] * output_adapter_down.shape[2]
    return pl.pallas_call(
        functools.partial(output_kernel, n),
        out_shape=jax.ShapeDtypeStruct((rows, span), BF16),
        in_specs=[in_vmem()] * 3 + [anywhere()] * 3,
        out_specs=in_vmem(),
        scratch_shapes=[
            pltpu.VMEM((KEY_VALUE_HEADS, rows, GROUP_HEADS * HEAD_SIZE), BF16),
            pltpu.VMEM((out_width, span), BF16),
            pltpu.VMEM((out_low_rows, span), BF16),
            pltpu.VMEM((out_low_rows, span), BF16),
            pltpu.VMEM((rows, span), F32),
        ]
        + low_scratch
        + [dma((3,))]
        + gather_semaphores(n)
        + [dma((n,))] * 4,
        compiler_params=pltpu.CompilerParams(
            collective_id=1, has_side_effects=True, vmem_limit_bytes=60 << 20
        ),
        cost_estimate=pl.CostEstimate(
            flops=2 * rows * out_width * span, bytes_accessed=20 << 20, transcendentals=0
        ),
    )(
        hidden,
        block_out,
        adapter,
        output_weight,
        low_table(output_adapter_down),
        up_table(output_adapter_up),
    )


def solution(mesh):
    placed = (
        P("groups", "tensor"),
        P(),
        P(None, "tensor"),
        P(None, "tensor"),
        P(None, "tensor"),
        P(None, "tensor", None),
        P(None, None, "tensor"),
        P(None, None, "tensor"),
        P(None, "tensor", None),
        P(None, None, "tensor"),
        P(("groups", "tensor"), None, None),
        P(("groups", "tensor"), None, None),
        P("groups", None),
        P("groups"),
    )
    return jax.shard_map(
        body, mesh=mesh, in_specs=placed, out_specs=P("groups", "tensor"), check_vma=False
    )
```

```python
import functools

import jax
import jax.numpy as jnp
from jax import lax
from jax.experimental import pallas as pl
from jax.experimental.pallas import tpu as pltpu
from jax.sharding import PartitionSpec as P

QUERY_HEADS = 64
KEY_VALUE_HEADS = 8
HEAD_SIZE = 128
GROUP_HEADS = QUERY_HEADS // KEY_VALUE_HEADS

adapter_scale = 0.5
rope_base = 500000.0
norm_eps = 1e-05

MESH = pl.DeviceIdType.MESH
F32 = jnp.float32
BF16 = jnp.bfloat16
NT = (((1,), (1,)), ((), ()))


def remote(src, dst, send_sem, recv_sem, peer):
    return pltpu.make_async_remote_copy(
        src_ref=src,
        dst_ref=dst,
        send_sem=send_sem,
        recv_sem=recv_sem,
        device_id={"tensor": peer},
        device_id_type=MESH,
    )


def greet_all(n, me):
    barrier = pltpu.get_barrier_semaphore()

    def greet(i, carry):
        pl.semaphore_signal(
            barrier, inc=1, device_id={"tensor": lax.rem(me + i, n)}, device_id_type=MESH
        )
        return carry

    lax.fori_loop(1, n, greet, 0)
    pl.semaphore_wait(barrier, n - 1)


def for_peers(n, me, action):
    def step(i, carry):
        action(i, lax.rem(me + i, n))
        return carry

    lax.fori_loop(1, n, step, 0)


class Exchange:
    def __init__(self, n, me, buf, send, recv, source):
        self.n, self.me, self.buf, self.send, self.recv, self.source = n, me, buf, send, recv, source

    def copy(self, i, peer):
        return remote(
            self.source(peer), self.buf.at[self.me], self.send.at[i], self.recv.at[self.me], peer
        )

    def start(self):
        for_peers(self.n, self.me, lambda i, peer: self.copy(i, peer).start())

    def wait_arrived(self):
        def arrived(i, peer):
            remote(
                self.source(peer), self.buf.at[peer], self.send.at[i], self.recv.at[peer], peer
            ).wait_recv()

        for_peers(self.n, self.me, arrived)

    def wait_sent(self):
        for_peers(self.n, self.me, lambda i, peer: self.copy(i, peer).wait_send())


class Gather:
    def __init__(self, n, me, view, zsend, ysend, csend, recv):
        self.wide = 2 if n % 4 == 0 and n <= 16 else 1
        self.depth = n // (2 * self.wide)
        self.view, self.me = view, me
        self.zsend, self.ysend, self.csend, self.recv = zsend, ysend, csend, recv
        self.core = lax.rem(me, 2)
        self.side = lax.rem(me // 2, self.wide)
        self.level = me // (2 * self.wide)

    def index(self, level, side, core):
        return (level * self.wide + side) * 2 + core

    def copy(self, block, send_sem, peer):
        return remote(self.view(block), self.view(block), send_sem, self.recv.at[block], peer)

    def up(self, d):
        block = self.index(self.level - d, self.side, self.core)
        return self.copy(block, self.zsend.at[0, d], self.index(self.level + 1, self.side, self.core))

    def down(self, d):
        block = self.index(self.level + d, self.side, self.core)
        return self.copy(block, self.zsend.at[1, d], self.index(self.level - 1, self.side, self.core))

    def across(self, level, sem):
        block = self.index(level, self.side, self.core)
        return self.copy(block, self.ysend.at[sem], self.index(self.level, 1 - self.side, self.core))

    def over(self, level, side, sem):
        block = self.index(level, side, self.core)
        return self.copy(
            block, self.csend.at[side, sem], self.index(self.level, self.side, 1 - self.core)
        )

    def await_block(self, block, peer):
        self.copy(block, self.zsend.at[0, 0], peer).wait_recv()

    def each_sign(self, d, action):
        @pl.when(self.level - d >= 0)
        def _():
            action(self.level - d, 0)

        @pl.when((d > 0) & (self.level + d < self.depth))
        def _():
            action(self.level + d, 1)

    def line(self, d):
        def low(level, sign):
            @pl.when(d > 0)
            def _():
                other = self.level - 1 if sign == 0 else self.level + 1
                self.await_block(
                    self.index(level, self.side, self.core),
                    self.index(other, self.side, self.core),
                )

            if sign == 0:

                @pl.when(self.level + 1 < self.depth)
                def _():
                    self.up(d).start()

                @pl.when((d == 0) & (self.level > 0))
                def _():
                    self.down(d).start()

            else:

                @pl.when(self.level > 0)
                def _():
                    self.down(d).start()

            if self.wide == 2:
                self.across(level, 2 * d + sign).start()
            self.over(level, self.side, 2 * d + sign).start()

        self.each_sign(d, low)

    def rest(self, d):
        def take(level, sign):
            if self.wide == 2:
                self.await_block(
                    self.index(level, 1 - self.side, self.core),
                    self.index(self.level, 1 - self.side, self.core),
                )
                self.over(level, 1 - self.side, 2 * d + sign).start()

        self.each_sign(d, take)

        def other(level, sign):
            for side in range(self.wide):
                self.await_block(
                    self.index(level, side, 1 - self.core),
                    self.index(self.level, self.side, 1 - self.core),
                )

        self.each_sign(d, other)

    def wait_sent(self):
        def step(d, carry):
            def sent(level, sign):
                if sign == 0:

                    @pl.when(self.level + 1 < self.depth)
                    def _():
                        self.up(d).wait_send()

                    @pl.when((d == 0) & (self.level > 0))
                    def _():
                        self.down(d).wait_send()

                else:

                    @pl.when(self.level > 0)
                    def _():
                        self.down(d).wait_send()

                if self.wide == 2:
                    self.across(level, 2 * d + sign).wait_send()
                for side in range(self.wide):
                    self.over(level, side, 2 * d + sign).wait_send()

            self.each_sign(d, sent)
            return carry

        lax.fori_loop(0, self.depth, step, 0)

    def each_chip(self, d, action):
        def step(i, carry):
            level = jnp.where(i < self.wide, self.level - d, self.level + d)
            side = lax.rem(i, self.wide)

            @pl.when((level >= 0) & (level < self.depth) & ((i < self.wide) | (d > 0)))
            def _():
                action(level * self.wide + side)

            return carry

        lax.fori_loop(0, 2 * self.wide, step, 0)


def gather_semaphores(n):
    return [
        pltpu.SemaphoreType.DMA((2, n)),
        pltpu.SemaphoreType.DMA((2 * n,)),
        pltpu.SemaphoreType.DMA((2, 2 * n)),
        pltpu.SemaphoreType.DMA((n,)),
    ]


def low_partial(values, down, adapter, low):
    rank = HEAD_SIZE // 2
    lanes = lax.broadcasted_iota(jnp.int32, (values.shape[0], HEAD_SIZE), 1) // rank
    low[...] = jnp.zeros_like(low)
    width = 4 * HEAD_SIZE

    def step(i, carry):
        spread = lax.dot_general(
            values, down[pl.ds(pl.multiple_of(i * width, width), width), :], NT,
            preferred_element_type=F32,
        )
        total = low[...]
        for part in range(width // HEAD_SIZE):
            mine = adapter == lanes + (i * (width // rank) + part * (HEAD_SIZE // rank))
            total = total + jnp.where(mine, spread[:, part * HEAD_SIZE : (part + 1) * HEAD_SIZE], 0.0)
        low[...] = total
        return carry

    lax.fori_loop(0, down.shape[0] // width, step, 0)


def low_upward(low, tables, adapter, totals):
    rank = HEAD_SIZE // 2
    lanes = lax.broadcasted_iota(jnp.int32, low.shape, 1) // rank
    width = 4 * HEAD_SIZE

    def step(i, carry):
        parts = []
        for part in range(width // HEAD_SIZE):
            mine = adapter == lanes + (i * (width // rank) + part * (HEAD_SIZE // rank))
            parts.append(jnp.where(mine, low, 0.0).astype(BF16))
        spread = jnp.concatenate(parts, axis=1)
        at = pl.ds(pl.multiple_of(i * width, width), width)
        for table, total in zip(tables, totals):
            total[...] += adapter_scale * jnp.dot(spread, table[at, :], preferred_element_type=F32)
        return carry

    lax.fori_loop(0, tables[0].shape[0] // width, step, 0)


def reduce_low(n, me, pieces, low_all):
    total = pieces[0]
    for i in range(1, n):
        total = total + pieces[i]
    total = total + pltpu.roll(total, HEAD_SIZE // 2, 1)
    low_all[me] = total.astype(BF16).astype(F32)


def project_kernel(
    n,
    hidden, gain, facts, cosine, sine,
    wq_hbm, wkv_hbm, down_hbm, upq_hbm, upkv_hbm, keys_hbm, values_hbm,
    block_out,
    q_out, kv_out, keys, values_ref, q_rows, new_keys, new_values, heads_out, buf, wq, wkv, down, upq, upkv, acc_q, acc_kv, stat, inv, own, low, pieces, low_all, q_cut, kv_cut,
    load_sem, zsend, ysend, csend, grecv, st_send, st_recv, rs_send, rs_recv, lo_send, lo_recv,
    q_send, q_recv, kv_send, kv_recv,
):
    me = lax.axis_index("tensor")
    rows, span = hidden.shape
    loads = [
        pltpu.make_async_copy(src, dst, load_sem.at[i])
        for i, (src, dst) in enumerate(
            [(down_hbm, down), (wq_hbm, wq), (wkv_hbm, wkv), (upq_hbm, upq), (upkv_hbm, upkv),
             (keys_hbm, keys), (values_hbm, values_ref)]
        )
    ]
    for load in loads[:5]:
        load.start()
    buf[me] = hidden[...]
    greet_all(n, me)
    gather = Gather(n, me, lambda block: buf.at[block], zsend, ysend, csend, grecv)
    gather.line(0)

    own_values = hidden[...].astype(F32)
    squares = jnp.sum(own_values * own_values, axis=1, keepdims=True)
    stat[me] = jnp.transpose(jnp.broadcast_to(squares, (rows, HEAD_SIZE)))[:8, :]
    stats = Exchange(n, me, stat, st_send, st_recv, lambda peer: stat.at[me])
    stats.start()
    acc_q[...] = jnp.zeros_like(acc_q)
    acc_kv[...] = jnp.zeros_like(acc_kv)
    stats.wait_arrived()
    total = stat[0]
    for i in range(1, n):
        total = total + stat[i]
    mean = total[0:1, :] / (n * span)
    scale = lax.rsqrt(mean + norm_eps)
    inv[...] = jnp.transpose(jnp.broadcast_to(scale, (HEAD_SIZE, rows)))

    def normed(block):
        return (
            buf[block].astype(F32) * inv[:, 0:1] * gain[:, pl.ds(pl.multiple_of(block * span, span), span)].astype(F32)
        ).astype(BF16)

    who = facts[:, 0:1]
    own[...] = normed(me)
    loads[0].wait()
    low_partial(own[...], down, who, low)
    piece = rows // n
    pieces[me] = low[pl.ds(pl.multiple_of(me * piece, 8), piece), :]
    reduce = Exchange(
        n, me, pieces, rs_send, rs_recv,
        lambda peer: low.at[pl.ds(pl.multiple_of(peer * piece, 8), piece), :],
    )
    reduce.start()
    spread = Exchange(n, me, low_all, lo_send, lo_recv, lambda peer: low_all.at[me])
    def step(d, carry):
        @pl.when(d + 1 < gather.depth)
        def _():
            gather.line(d + 1)

        @pl.when(d == 1)
        def _():
            reduce.wait_arrived()
            reduce_low(n, me, pieces, low_all)
            spread.start()

        @pl.when(d == 2)
        def _():
            spread.wait_arrived()
            low_upward(low_all[...].reshape(rows, HEAD_SIZE), [upq, upkv], who, [acc_q, acc_kv])

        gather.rest(d)

        @pl.when(d == 0)
        def _():
            for load in loads[1:5]:
                load.wait()
            for load in loads[5:]:
                load.start()

        def chip_part(chip):
            for core in range(2):
                block = chip * 2 + core
                values = normed(block)
                at = pl.ds(pl.multiple_of(block * span, span), span)
                acc_q[...] += jnp.dot(values, wq[at, :], preferred_element_type=F32)
                acc_kv[...] += jnp.dot(values, wkv[at, :], preferred_element_type=F32)

        gather.each_chip(d, chip_part)
        return carry

    lax.fori_loop(0, gather.depth, step, 0)

    row_blocks = n // KEY_VALUE_HEADS
    block_rows = rows // row_blocks
    slots = acc_q.shape[1] // HEAD_SIZE
    cos, sin = cosine[...], sine[...]
    kv_cut[...] = acc_kv[...].astype(BF16)
    kv_group = me // row_blocks

    def kv_copy(part):
        peer = kv_group * row_blocks + part
        slot = lax.rem(me, row_blocks)
        return peer, slot, remote(
            kv_cut.at[pl.ds(part * block_rows, block_rows), :], kv_out.at[slot],
            kv_send.at[part], kv_recv.at[slot], peer,
        )

    def q_copy(i, part):
        column = me * slots + i
        peer = lax.rem(column, KEY_VALUE_HEADS) * row_blocks + part
        slot = column // KEY_VALUE_HEADS
        return peer, slot, remote(
            q_cut.at[i, pl.ds(part * block_rows, block_rows), :], q_out.at[slot],
            q_send.at[i, part], q_recv.at[slot], peer,
        )

    for part in range(row_blocks):
        peer, slot, copy = kv_copy(part)

        @pl.when(peer != me)
        def _():
            copy.start()

        @pl.when(peer == me)
        def _():
            kv_out[slot] = kv_cut[pl.ds(part * block_rows, block_rows), :]

    for i in range(slots):
        values = acc_q[:, i * HEAD_SIZE : (i + 1) * HEAD_SIZE]
        q_cut[i] = (values * cos + pltpu.roll(values, HEAD_SIZE // 2, 1) * sin).astype(BF16)
        for part in range(row_blocks):
            peer, slot, copy = q_copy(i, part)

            @pl.when(peer != me)
            def _():
                copy.start()

            @pl.when(peer == me)
            def _():
                q_out[slot] = q_cut[i, pl.ds(part * block_rows, block_rows), :]

    stats.wait_sent()
    reduce.wait_sent()
    spread.wait_sent()
    gather.wait_sent()
    for part in range(row_blocks):
        peer, slot, copy = kv_copy(part)

        @pl.when(peer != me)
        def _():
            copy.wait_send()
            remote(
                kv_cut.at[pl.ds(part * block_rows, block_rows), :], kv_out.at[part],
                kv_send.at[part], kv_recv.at[part], peer,
            ).wait_recv()

    for i in range(slots):
        for part in range(row_blocks):
            peer, slot, copy = q_copy(i, part)

            @pl.when(peer != me)
            def _():
                copy.wait_send()

    for slot in range(GROUP_HEADS):
        sender = (slot * KEY_VALUE_HEADS + kv_group) // slots

        @pl.when(sender != me)
        def _():
            remote(
                q_cut.at[0, pl.ds(0, block_rows), :], q_out.at[slot],
                q_send.at[0, 0], q_recv.at[slot], sender,
            ).wait_recv()

    first_row = lax.rem(me, row_blocks) * block_rows
    block_at = pl.ds(pl.multiple_of(first_row, block_rows), block_rows)
    fresh = jnp.concatenate([kv_out[i] for i in range(row_blocks)], axis=1).astype(F32)
    fresh_key = fresh[:, :HEAD_SIZE]
    new_keys[...] = (
        fresh_key * cosine[block_at, :]
        + pltpu.roll(fresh_key, HEAD_SIZE // 2, 1) * sine[block_at, :]
    ).astype(BF16).astype(F32)
    new_values[...] = fresh[:, HEAD_SIZE:]
    for slot in range(GROUP_HEADS):
        q_rows[:, slot, :] = q_out[slot].astype(F32)
    loads[5].wait()
    loads[6].wait()
    group = 16
    cache_len = keys.shape[1]
    place = lax.broadcasted_iota(jnp.int32, (group, GROUP_HEADS, cache_len), 2)
    factor = HEAD_SIZE ** (-0.5)

    def some_rows(i, carry):
        at = pl.ds(pl.multiple_of(i * group, group), group)
        queries = q_rows[at]
        ends = facts[pl.ds(pl.multiple_of(first_row + i * group, group), group), :]
        ends = ends[:, None, :][:, :, HEAD_SIZE // 2 : HEAD_SIZE // 2 + 1]
        scores = factor * lax.dot_general(
            queries.astype(BF16), keys[at], (((2,), (2,)), ((0,), (0,))),
            preferred_element_type=F32,
        )
        scores = jnp.where(place < ends, scores, -jnp.inf)
        own_score = factor * jnp.sum(queries * new_keys[at][:, None, :], axis=2, keepdims=True)
        highest = jnp.maximum(jnp.max(scores, axis=2, keepdims=True), own_score)
        weights = jnp.exp(scores - highest)
        own_weight = jnp.exp(own_score - highest)
        share = 1.0 / (jnp.sum(weights, axis=2, keepdims=True) + own_weight)
        heads = lax.dot_general(
            (weights * share).astype(BF16), values_ref[at], (((2,), (1,)), ((0,), (0,))),
            preferred_element_type=F32,
        )
        own_prob = (own_weight * share).astype(BF16).astype(F32)
        heads_out[at] = heads + own_prob * new_values[at][:, None, :]
        return carry

    lax.fori_loop(0, block_rows // group, some_rows, 0)
    for slot in range(GROUP_HEADS):
        block_out[:, slot * HEAD_SIZE : (slot + 1) * HEAD_SIZE] = heads_out[:, slot, :].astype(BF16)


def output_kernel(
    n,
    hidden, attended, facts, wo_hbm, down_hbm, up_hbm,
    result,
    buf, wo, down, up, acc, low, pieces, low_all,
    load_sem, zsend, ysend, csend, grecv, rs_send, rs_recv, lo_send, lo_recv,
):
    me = lax.axis_index("tensor")
    rows, span = hidden.shape
    block_rows, width = attended.shape
    row_blocks = rows // block_rows
    loads = [
        pltpu.make_async_copy(src, dst, load_sem.at[i])
        for i, (src, dst) in enumerate([(down_hbm, down), (wo_hbm, wo), (up_hbm, up)])
    ]
    for load in loads:
        load.start()

    def at_block(block):
        return (
            block // row_blocks,
            pl.ds(pl.multiple_of(lax.rem(block, row_blocks) * block_rows, block_rows), block_rows),
        )

    kv_group, own_rows = at_block(me)
    buf[kv_group, own_rows, :] = attended[...]
    acc[...] = hidden[...].astype(F32)
    greet_all(n, me)

    def view(block):
        group, at = at_block(block)
        return buf.at[group, at, :]

    gather = Gather(n, me, view, zsend, ysend, csend, grecv)
    gather.line(0)
    who = facts[:, 0:1]
    piece = rows // n
    reduce = Exchange(
        n, me, pieces, rs_send, rs_recv,
        lambda peer: low.at[pl.ds(pl.multiple_of(peer * piece, 8), piece), :],
    )
    spread = Exchange(n, me, low_all, lo_send, lo_recv, lambda peer: low_all.at[me])

    def first_low():
        first = pl.multiple_of(lax.rem(me, row_blocks) * span, span)
        low_partial(buf[kv_group, :, pl.ds(first, span)], down, who, low)
        pieces[me] = low[pl.ds(pl.multiple_of(me * piece, 8), piece), :]
        reduce.start()

    def second_low():
        reduce.wait_arrived()
        reduce_low(n, me, pieces, low_all)
        spread.start()

    def third_low():
        spread.wait_arrived()
        low_upward(low_all[...].reshape(rows, HEAD_SIZE), [up], who, [acc])

    early = row_blocks == 2

    def step(d, carry):
        @pl.when(d + 1 < gather.depth)
        def _():
            gather.line(d + 1)

        if early:
            pl.when(d == 1)(second_low)
            pl.when(d == 2)(third_low)
        gather.rest(d)

        @pl.when(d == 0)
        def _():
            for load in loads:
                load.wait()

        if early:
            pl.when(d == 0)(first_low)

        def chip_part(chip):
            block = chip * 2
            group = block // row_blocks
            first = pl.multiple_of(lax.rem(block, row_blocks) * block_rows, block_rows)
            at = pl.ds(first, 2 * block_rows)
            acc[at, :] += jnp.dot(
                buf[group, at, :], wo[pl.ds(pl.multiple_of(group * width, width), width), :],
                preferred_element_type=F32,
            )

        gather.each_chip(d, chip_part)
        return carry

    lax.fori_loop(0, gather.depth, step, 0)
    if not early:
        first_low()
        second_low()
        third_low()
    result[...] = acc[...]
    reduce.wait_sent()
    spread.wait_sent()
    gather.wait_sent()


def rotate_tables(positions):
    half_width = HEAD_SIZE // 2
    entry = jnp.arange(HEAD_SIZE, dtype=jnp.int32)
    frequency = rope_base ** (-((entry % half_width).astype(F32) * 2.0) / HEAD_SIZE)
    angles = positions.astype(F32)[:, None] * frequency[None, :]
    sign = jnp.where(entry < half_width, -1.0, 1.0).astype(F32)
    return jnp.cos(angles), jnp.sin(angles) * sign[None, :]


def in_vmem():
    return pl.BlockSpec(memory_space=pltpu.VMEM)


def anywhere():
    return pl.BlockSpec(memory_space=pl.ANY)


def body(
    hidden,
    attention_norm_gain,
    query_weight,
    key_value_weight,
    output_weight,
    adapter_down_factors,
    adapter_query_up,
    adapter_key_value_up,
    output_adapter_down,
    output_adapter_up,
    key_cache,
    value_cache,
    adapter,
    lengths,
):
    n = lax.axis_size("tensor")
    rows, span = hidden.shape
    kv_width = key_value_weight.shape[1]
    row_blocks = n // KEY_VALUE_HEADS
    block_rows = rows // row_blocks
    slots = span // HEAD_SIZE
    dma = pltpu.SemaphoreType.DMA
    cosine, sine = rotate_tables(lengths)
    first_half = jnp.arange(HEAD_SIZE, dtype=jnp.int32)[None, :] < HEAD_SIZE // 2
    facts = jnp.where(first_half, adapter, lengths[:, None])

    def low_table(table):
        return jnp.swapaxes(table, 1, 2).reshape(-1, table.shape[1])

    def up_table(table):
        return table.reshape(-1, table.shape[2])

    low_rows = adapter_down_factors.shape[0] * adapter_down_factors.shape[2]
    width = query_weight.shape[0]
    low_scratch = [
        pltpu.VMEM((rows, HEAD_SIZE), F32),
        pltpu.VMEM((n, rows // n, HEAD_SIZE), F32),
        pltpu.VMEM((n, rows // n, HEAD_SIZE), F32),
    ]
    block_out = pl.pallas_call(
        functools.partial(project_kernel, n),
        out_shape=jax.ShapeDtypeStruct((block_rows, GROUP_HEADS * HEAD_SIZE), BF16),
        in_specs=[in_vmem()] * 5 + [anywhere()] * 7,
        out_specs=in_vmem(),
        scratch_shapes=[
            pltpu.VMEM((GROUP_HEADS, block_rows, HEAD_SIZE), BF16),
            pltpu.VMEM((row_blocks, block_rows, kv_width), BF16),
            pltpu.VMEM(key_cache.shape, BF16),
            pltpu.VMEM(value_cache.shape, BF16),
            pltpu.VMEM((block_rows, GROUP_HEADS, HEAD_SIZE), F32),
            pltpu.VMEM((block_rows, HEAD_SIZE), F32),
            pltpu.VMEM((block_rows, HEAD_SIZE), F32),
            pltpu.VMEM((block_rows, GROUP_HEADS, HEAD_SIZE), F32),
            pltpu.VMEM((n, rows, span), BF16),
            pltpu.VMEM((width, span), BF16),
            pltpu.VMEM((width, kv_width), BF16),
            pltpu.VMEM((low_rows, span), BF16),
            pltpu.VMEM((low_rows, span), BF16),
            pltpu.VMEM((low_rows, kv_width), BF16),
            pltpu.VMEM((rows, span), F32),
            pltpu.VMEM((rows, kv_width), F32),
            pltpu.VMEM((n, 8, rows), F32),
            pltpu.VMEM((rows, HEAD_SIZE), F32),
            pltpu.VMEM((rows, span), BF16),
        ]
        + low_scratch
        + [
            pltpu.VMEM((slots, rows, HEAD_SIZE), BF16),
            pltpu.VMEM((rows, kv_width), BF16),
            dma((7,)),
        ]
        + gather_semaphores(n)
        + [dma((n,))] * 6
        + [dma((slots, row_blocks)), dma((GROUP_HEADS,)), dma((row_blocks,)), dma((row_blocks,))],
        compiler_params=pltpu.CompilerParams(
            collective_id=0, has_side_effects=True, vmem_limit_bytes=63 << 20
        ),
        cost_estimate=pl.CostEstimate(
            flops=2 * rows * width * (span + kv_width), bytes_accessed=24 << 20, transcendentals=0
        ),
    )(
        hidden,
        attention_norm_gain.reshape(1, n * span),
        facts,
        cosine,
        sine,
        query_weight,
        key_value_weight,
        low_table(adapter_down_factors),
        up_table(adapter_query_up),
        up_table(adapter_key_value_up),
        key_cache,
        value_cache,
    )

    out_width = output_weight.shape[0]
    out_low_rows = output_adapter_down.shape[0] * output_adapter_down.shape[2]
    return pl.pallas_call(
        functools.partial(output_kernel, n),
        out_shape=jax.ShapeDtypeStruct((rows, span), F32),
        in_specs=[in_vmem()] * 3 + [anywhere()] * 3,
        out_specs=in_vmem(),
        scratch_shapes=[
            pltpu.VMEM((KEY_VALUE_HEADS, rows, GROUP_HEADS * HEAD_SIZE), BF16),
            pltpu.VMEM((out_width, span), BF16),
            pltpu.VMEM((out_low_rows, span), BF16),
            pltpu.VMEM((out_low_rows, span), BF16),
            pltpu.VMEM((rows, span), F32),
        ]
        + low_scratch
        + [dma((3,))]
        + gather_semaphores(n)
        + [dma((n,))] * 4,
        compiler_params=pltpu.CompilerParams(
            collective_id=1, has_side_effects=True, vmem_limit_bytes=60 << 20
        ),
        cost_estimate=pl.CostEstimate(
            flops=2 * rows * out_width * span, bytes_accessed=20 << 20, transcendentals=0
        ),
    )(
        hidden,
        block_out,
        facts,
        output_weight,
        low_table(output_adapter_down),
        up_table(output_adapter_up),
    ).astype(BF16)


def solution(mesh):
    placed = (
        P("groups", "tensor"),
        P(),
        P(None, "tensor"),
        P(None, "tensor"),
        P(None, "tensor"),
        P(None, "tensor", None),
        P(None, None, "tensor"),
        P(None, None, "tensor"),
        P(None, "tensor", None),
        P(None, None, "tensor"),
        P(("groups", "tensor"), None, None),
        P(("groups", "tensor"), None, None),
        P("groups", None),
        P("groups"),
    )
    return jax.shard_map(
        body, mesh=mesh, in_specs=placed, out_specs=P("groups", "tensor"), check_vma=False
    )
```
